256 devices in a mesh: ctx: 8 (over x_hi, y), fsdp: 32 (over z, x_lo, core).
Axes of the slice: x: 4 (x_hi: 2, x_lo: 2; x = x_hi * 2 + x_lo), y: 4, z: 8, core: 2. Of those that a mesh axis runs over, the one named last changes fastest.
Arguments:
- query_a: bfloat16 [32, 1024, 2048], P('fsdp', 'ctx'), may hold values from -64 to 64
- key_a: bfloat16 [32, 1024, 256], P('fsdp', 'ctx'), may hold values from -8 to 8
- value_a: bfloat16 [32, 1024, 256], P('fsdp', 'ctx'), may hold values from -6 to 6
- resid_in: bfloat16 [32, 1024, 1440], P('fsdp', 'ctx'), may hold values from -6 to 6
- doc_lengths: int32 [32, 6], P('fsdp'), may hold values from 1 to 768, 1024 in all within a row
- w_out: bfloat16 [2048, 1440], P('fsdp'), may hold values from -0.125 to 0.125
- w_qkv: bfloat16 [1440, 2560], P('fsdp'), may hold values from -8 to 8
- grad_out: bfloat16 [32, 1024, 2048], P('fsdp', 'ctx'), may hold values from -6 to 6
- grad_resid: bfloat16 [32, 1024, 1440], P('fsdp', 'ctx'), may hold values from -8 to 8
Outputs:
- banded_out: bfloat16 [32, 1024, 2048], P('fsdp', 'ctx')
- grad_input: bfloat16 [32, 1024, 1440], P('fsdp', 'ctx')
- grad_query: bfloat16 [32, 1024, 2048], P('fsdp', 'ctx')
- grad_key: bfloat16 [32, 1024, 256], P('fsdp', 'ctx')
- grad_value: bfloat16 [32, 1024, 256], P('fsdp', 'ctx')
- grad_w_out: float32 [2048, 1440], P('fsdp')
- grad_w_qkv: float32 [1440, 2560], P('fsdp')
The draws below stay inside these ranges and needn't reach their ends.
Inputs may be any that keep to these rules, and one draw needn't show every extreme that they name: `doc_lengths`: the lengths of a sequence sum to 1024, and one document has 768 positions.
All inputs are finite; a program needn't handle non-finite values.
Results may differ from the reference program's by a relative error of at most 0.03.
Values may be sent and summed in bfloat16 or wider, within the bound.
No kernel may reach another device: no remote copies, remote signals or barrier semaphores. Data moves between devices by JAX's collectives and lax.ppermute only.
A program may use at most 128 MiB of HBM per device.

```python
import math
import jax
import jax.numpy as jnp
import numpy as np
from jax import lax

H = 32
KV = 4
DH = 64
D = 1440
BAND = 128
DOCS = 6
TOK_DEV = 128
SEQ = 1024
SEQS = 32
N_CTX = 8


def drawn_pair(key):
    key_query, key_keys = jax.random.split(key, 2)
    shape_query = (SEQS, SEQ, H * DH)
    shape_keys = (SEQS, SEQ, KV * DH)
    query = jax.random.truncated_normal(key_query, -4.0, 4.0, shape_query, jnp.float32)
    keys = jax.random.truncated_normal(key_keys, -4.0, 4.0, shape_keys, jnp.float32)
    return (query.astype(jnp.bfloat16), keys.astype(jnp.bfloat16))


def draw_query_a(key, part):
    return drawn_pair(jax.random.fold_in(key, 7))[0]


def draw_key_a(key, part):
    return drawn_pair(jax.random.fold_in(key, 7))[1]


def draw_w_qkv(key, part):
    width = (H + 2 * KV) * DH
    matrix = jax.random.truncated_normal(key, -4.0, 4.0, (D, width), jnp.float32) * D ** (-0.5)
    return matrix.astype(jnp.bfloat16)


def draw_grad_resid(key, part):
    key_common, key_rough = jax.random.split(jax.random.fold_in(key, 11))
    common = 0.8 * jax.random.normal(key_common, (SEQS, 1, D), jnp.float32)
    rough = jax.random.normal(key_rough, (SEQS, SEQ, D), jnp.float32)
    return jnp.clip(common + rough, -7.5, 7.5).astype(jnp.bfloat16)


def level_of(key, dims, cuts, low, largest):
    loudness, own = 1.0, jax.random.fold_in(key, 6)
    for position, blocks in cuts:
        draws = jnp.exp(jax.random.uniform(jax.random.fold_in(own, position), (blocks,), jnp.float32, low / len(cuts), largest / len(cuts)))
        loudness = loudness * jnp.repeat(draws, dims[position] // blocks).reshape([-1 if axis == position else 1 for axis in range(len(dims))])
    return loudness


def length_profile(number_of, total, bound, lean):
    loads = [(1 << 20) // math.isqrt(standing ** lean) + 1 for standing in range(2, number_of + 1)]
    surplus, counts = total - bound - (number_of - 1), [1] * (number_of - 1)
    while surplus > 0:
        candidates = [i for i in range(number_of - 1) if counts[i] < bound]
        whole, remaining = sum([loads[i] for i in candidates]), surplus
        for i in candidates:
            extra = min(bound - counts[i], max(1, remaining * loads[i] // whole), surplus)
            counts[i] = counts[i] + extra
            surplus = surplus - extra
    return np.array([bound] + counts)


def ragged(own_key, amount, total, most, skew):
    if amount == 2:
        one = jax.random.randint(own_key, (), max(1, total - most), min(most, total - 1) + 1)
        return jnp.stack([one, total - one])
    sizes = jnp.asarray(length_profile(amount, total, most, skew), jnp.int32)
    twos = (amount - 1) // 2
    source_of, receiver = sizes[1:1 + 2 * twos:2], sizes[2:2 + 2 * twos:2]
    margin = jnp.minimum(source_of - 1, most - receiver)
    shifted = jax.random.randint(jax.random.fold_in(own_key, 1), (twos,), 0, 1 << 20) % (margin + 1)
    sizes = sizes.at[1:1 + 2 * twos:2].set(source_of - shifted).at[2:2 + 2 * twos:2].set(receiver + shifted)
    return sizes[jax.random.permutation(jax.random.fold_in(own_key, 2), amount)]


def normal_values(stream_key, extent, deviation, bound, cuts=(), kind=jnp.bfloat16):
    values = jax.random.normal(stream_key, extent, jnp.float32) * deviation
    if len(cuts) > 0:
        values = level_of(stream_key, extent, cuts, -0.22, 0.18) * values
    return jnp.clip(values, min=-bound, max=bound).astype(kind)


def setup_inputs(seed: int = 0) -> dict:
    key_of = jax.random.split(jax.random.key(seed), 10)
    query_a = draw_query_a(jax.random.fold_in(key_of[9], 71), 0)
    key_a = draw_key_a(jax.random.fold_in(key_of[9], 71), 0)
    value_a = normal_values(key_of[2], (SEQS, SEQ, KV * DH), 1.0, 6.0, ((0, 32), (1, 8)))
    resid_in = normal_values(key_of[3], (SEQS, SEQ, D), 1.0, 6.0, ((0, 32), (1, 8)))
    doc_lengths = jax.vmap(lambda own: ragged(own, DOCS, SEQ, 3 * SEQ // 4, 2))(jax.random.split(key_of[4], SEQS)).reshape((SEQS, DOCS)).astype(jnp.int32)
    w_out = normal_values(key_of[5], (H * DH, D), (H * DH) ** -0.5, 0.125, ((0, 32),))
    w_qkv = draw_w_qkv(jax.random.fold_in(key_of[9], 71), 0)
    grad_out = normal_values(key_of[7], (SEQS, SEQ, H * DH), 1.0, 6.0, ((0, 32), (1, 8)))
    grad_resid = draw_grad_resid(jax.random.fold_in(key_of[9], 71), 0)
    return dict(query_a=query_a, key_a=key_a, value_a=value_a, resid_in=resid_in, doc_lengths=doc_lengths, w_out=w_out, w_qkv=w_qkv, grad_out=grad_out, grad_resid=grad_resid)


MASKED = -1e+30
EPSILON = 1e-05

def doc_index(lengths):
    ends = jnp.cumsum(lengths)
    places = jnp.arange(SEQ, dtype=jnp.int32)
    return lax.optimization_barrier(jnp.sum((places[:, None] >= ends[None, :]).astype(jnp.int32), axis=1))

def allowed_pairs(documents, reach):
    places = jnp.arange(SEQ, dtype=jnp.int32)
    behind = places[:, None] - places[None, :]
    same_doc = documents[:, None] == documents[None, :]
    return same_doc & (behind >= 0) & (behind < reach)

def query_heads(rows):
    return rows.reshape(SEQ, KV, H // KV, DH).transpose(1, 2, 0, 3)

def pair_heads(rows):
    return rows.reshape(SEQ, KV, DH).transpose(1, 0, 2)

def merge_query(heads):
    return heads.transpose(2, 0, 1, 3).reshape(SEQ, H * DH)

def merge_pair(heads):
    return heads.transpose(1, 0, 2).reshape(SEQ, KV * DH)

def attention_weights(query_group, key_head, allowed):
    scores = jnp.einsum('gid,jd->gij', query_group.astype(jnp.float32), key_head.astype(jnp.float32)) * DH ** (-0.5)
    scores = jnp.where(allowed, scores, MASKED)
    row_max = lax.optimization_barrier(jnp.max(scores, axis=-1, keepdims=True))
    log_total = row_max + jnp.log(lax.optimization_barrier(jnp.sum(jnp.where(allowed, jnp.exp(scores - row_max), 0.0), axis=-1, keepdims=True)))
    return jnp.where(allowed, jnp.exp(scores - log_total), 0.0)

def attend(query, keys, values, allowed):

    def one_head(items):
        query_group, key_head, value_head = items
        weights = attention_weights(query_group, key_head, allowed).astype(jnp.bfloat16)
        summed = jnp.einsum('gij,jd->gid', weights.astype(jnp.float32), value_head.astype(jnp.float32))
        return summed.astype(jnp.bfloat16)
    return merge_query(lax.map(one_head, (query_heads(query), pair_heads(keys), pair_heads(values))))

def attend_back(query, keys, values, output, grad, allowed):

    def one_head(items):
        query_group, key_head, value_head, out_group, grad_group = items
        weights = attention_weights(query_group, key_head, allowed)
        weights_bf = weights.astype(jnp.bfloat16)
        grad_weights = jnp.einsum('gid,jd->gij', grad_group.astype(jnp.float32), value_head.astype(jnp.float32))
        correction = lax.optimization_barrier(jnp.sum(grad_group.astype(jnp.float32) * out_group.astype(jnp.float32), axis=-1, keepdims=True))
        grad_scores = (weights * (grad_weights - correction)).astype(jnp.bfloat16)
        grad_q = jnp.einsum('gij,jd->gid', grad_scores.astype(jnp.float32), key_head.astype(jnp.float32)) * DH ** (-0.5)
        grad_k = jnp.einsum('gij,gid->jd', grad_scores.astype(jnp.float32), query_group.astype(jnp.float32)) * DH ** (-0.5)
        grad_v = jnp.einsum('gij,gid->jd', weights_bf.astype(jnp.float32), grad_group.astype(jnp.float32))
        return (grad_q.astype(jnp.bfloat16), grad_k.astype(jnp.bfloat16), grad_v.astype(jnp.bfloat16))
    items = (query_heads(query), pair_heads(keys), pair_heads(values), query_heads(output), query_heads(grad))
    grad_q, grad_k, grad_v = lax.map(one_head, items)
    return (merge_query(grad_q), merge_pair(grad_k), merge_pair(grad_v))

def block_terms(left, right, total):
    left_blocks = left.reshape(N_CTX, TOK_DEV, left.shape[1])
    right_blocks = right.reshape(N_CTX, TOK_DEV, right.shape[1])

    def add_block(acc, pieces):
        left_piece, right_piece = pieces
        term = jnp.dot(left_piece.T, right_piece, preferred_element_type=jnp.float32).astype(jnp.bfloat16)
        term = lax.optimization_barrier(term)
        return (acc + term.astype(jnp.float32), None)
    total, unused = lax.scan(add_block, total, (left_blocks, right_blocks))
    return total

def reference(query_a, key_a, value_a, resid_in, doc_lengths, w_out, w_qkv, grad_out, grad_resid):

    def one_sequence(carry, items):
        sum_out, sum_qkv = carry
        query, keys, values, resid, lengths, grad_o, grad_r = items
        documents = doc_index(lengths)
        full_allowed = allowed_pairs(documents, SEQ)
        band_allowed = allowed_pairs(documents, BAND)
        attended = attend(query, keys, values, full_allowed)
        resid_mid = (resid.astype(jnp.float32) + jnp.dot(attended, w_out, preferred_element_type=jnp.float32)).astype(jnp.bfloat16)
        resid_f = resid_mid.astype(jnp.float32)
        inverse_rms = lax.rsqrt(lax.optimization_barrier(jnp.mean(resid_f * resid_f, axis=-1, keepdims=True)) + EPSILON)
        normed = resid_f * inverse_rms
        normed_bf = normed.astype(jnp.bfloat16)
        projected = jnp.dot(normed_bf, w_qkv, preferred_element_type=jnp.float32).astype(jnp.bfloat16)
        query_b = projected[:, :H * DH]
        key_b = projected[:, H * DH:H * DH + KV * DH]
        value_b = projected[:, H * DH + KV * DH:]
        banded = attend(query_b, key_b, value_b, band_allowed)
        grad_qb, grad_kb, grad_vb = attend_back(query_b, key_b, value_b, banded, grad_o, band_allowed)
        grad_proj = jnp.concatenate([grad_qb, grad_kb, grad_vb], axis=1)
        grad_normed = jnp.dot(grad_proj, w_qkv.T, preferred_element_type=jnp.float32)
        middle = lax.optimization_barrier(jnp.mean(grad_normed * normed, axis=-1, keepdims=True))
        grad_mid = (grad_r.astype(jnp.float32) + inverse_rms * (grad_normed - normed * middle)).astype(jnp.bfloat16)
        grad_attended = jnp.dot(grad_mid, w_out.T, preferred_element_type=jnp.float32).astype(jnp.bfloat16)
        grad_q, grad_k, grad_v = attend_back(query, keys, values, attended, grad_attended, full_allowed)
        sum_out = block_terms(attended, grad_mid, sum_out)
        sum_qkv = block_terms(normed_bf, grad_proj, sum_qkv)
        return ((sum_out, sum_qkv), (banded, grad_mid, grad_q, grad_k, grad_v))
    items = (query_a, key_a, value_a, resid_in, doc_lengths, grad_out, grad_resid)
    start = (jnp.zeros(w_out.shape, jnp.float32), jnp.zeros(w_qkv.shape, jnp.float32))
    (grad_w_out, grad_w_qkv), outputs = lax.scan(one_sequence, start, items)
    banded_out, grad_input, grad_query, grad_key, grad_value = outputs
    return (banded_out, grad_input, grad_query, grad_key, grad_value, grad_w_out, grad_w_qkv)
```

```python
import functools

import jax
import jax.numpy as jnp
import numpy as np
from jax import lax
from jax.experimental import pallas as pl
from jax.experimental.pallas import tpu as pltpu
from jax.sharding import PartitionSpec as P

H = 32
KV = 4
DH = 64
BAND = 128
ROWS = 128
SEQ = 1024
KB = 256
MASKED = -1e30
LOWEST = -1e29
EPSILON = 1e-05
SCALE = DH**-0.5
CTX = ("xh", "y")
FSDP = ("z", "xl", "c")
X = ("xh", "xl")
F32 = jnp.float32
BF16 = jnp.bfloat16
CUT = 1024
VMEM_LIMIT = 48 * 1024 * 1024


def nt(a, b):
    return lax.dot_general(a, b, (((1,), (1,)), ((), ())), preferred_element_type=F32)


def nn(a, b):
    return lax.dot_general(a, b, (((1,), (0,)), ((), ())), preferred_element_type=F32)


def tn(a, b):
    return lax.dot_general(a, b, (((0,), (0,)), ((), ())), preferred_element_type=F32)


def row_starts(len_ref, rows):
    start, end = jnp.zeros_like(rows), 0
    for d in range(6):
        size = len_ref[0, d]
        end = end + size
        start = start + jnp.where(rows >= end, size, 0)
    return start


def scalar_start(len_ref, row):
    start, end = 0, 0
    for d in range(6):
        size = len_ref[0, d]
        end = end + size
        start = start + jnp.where(row >= end, size, 0)
    return start


def both_lanes(block, s):
    wide = block.astype(F32)
    lane = lax.broadcasted_iota(jnp.int32, wide.shape, 1)
    mine = jnp.where((lane < DH) if s == 0 else (lane >= DH), wide, 0.0)
    other = pltpu.roll(mine, DH, 1)
    pair = (mine, other) if s == 0 else (other, mine)
    return jnp.concatenate(pair, axis=0).astype(BF16)


def stacked(ref, s, scale=None):
    parts = [ref[:, s * 512 + p * 128 : s * 512 + (p + 1) * 128] for p in range(4)]
    whole = jnp.concatenate(parts, axis=0)
    if scale is not None:
        whole = whole * jnp.asarray(scale, whole.dtype)
    return whole


def head_transposed(block, s):
    return jnp.transpose(block.astype(F32))[s * DH : (s + 1) * DH].astype(BF16)


def mask_of(starts, rows, first_key):
    keys = first_key + lax.broadcasted_iota(jnp.int32, (KB, ROWS), 0)
    allowed = (keys >= starts) & (keys <= rows)
    bias = jnp.where(allowed, 0.0, MASKED)
    return jnp.concatenate([bias] * 4, axis=1)


def corrections(grad_ref, out_ref, s):
    even, odd = [], []
    for p in range(4):
        at = slice(s * 512 + p * 128, s * 512 + (p + 1) * 128)
        prod = jnp.transpose(grad_ref[:, at].astype(F32) * out_ref[:, at].astype(F32))
        even.append(jnp.sum(prod[:DH], axis=0, keepdims=True))
        odd.append(jnp.sum(prod[DH:], axis=0, keepdims=True))
    return jnp.concatenate(even, axis=1), jnp.concatenate(odd, axis=1)


def store_rows(ref, transposed, s):
    for p in range(4):
        at = slice(s * 512 + p * 128, s * 512 + (p + 1) * 128)
        ref[:, at] = jnp.transpose(transposed[:, p * 128 : (p + 1) * 128]).astype(ref.dtype)


def head_pair(first, second):
    lane = lax.broadcasted_iota(jnp.int32, (KB, 128), 1)
    low = first[:KB] + pltpu.roll(first[KB:], DH, 1)
    high = pltpu.roll(second[:KB], DH, 1) + second[KB:]
    return jnp.where(lane < DH, low, high)


def full_forward_kernel(
    len_ref, ctx_ref, q_ref, k_ref, v_ref, early_a, early_b, ot_ref, lse_ref, acc, stat
):
    first_row = ctx_ref[0, 0] * ROWS
    rows = first_row + lax.broadcasted_iota(jnp.int32, (1, ROWS), 1)
    starts = row_starts(len_ref, rows)
    low = scalar_start(len_ref, first_row) // KB
    high = (first_row + ROWS + KB - 1) // KB
    acc[...] = jnp.zeros_like(acc)
    stat[:4] = jnp.full((4, 512), LOWEST, F32)
    stat[4:] = jnp.zeros((4, 512), F32)

    def block(b, carry):
        at = pl.ds(pl.multiple_of(b * KB, KB), KB)
        bias = mask_of(starts, rows, b * KB)
        keys, values = k_ref[at, :], v_ref[at, :]
        for s in range(2):
            scores = nt(both_lanes(keys, s), stacked(q_ref, s, SCALE))
            turned = head_transposed(values, s)
            for parity in range(2):
                n = s * 2 + parity
                part = scores[parity * KB : (parity + 1) * KB] + bias
                old = stat[n : n + 1]
                new = jnp.maximum(old, jnp.max(part, axis=0, keepdims=True))
                weights = jnp.exp(part - new)
                fade = jnp.exp(old - new)
                stat[n : n + 1] = new
                stat[4 + n : 5 + n] = stat[4 + n : 5 + n] * fade + jnp.sum(weights, axis=0, keepdims=True)
                acc[n] = acc[n] * fade + nn(turned, weights.astype(BF16))
        return carry

    lax.fori_loop(low, high, block, 0)
    lse_ref[0] = jnp.concatenate([stat[:4] + jnp.log(stat[4:]), jnp.zeros((4, 512), F32)], axis=0)
    for s in range(2):
        halves = [acc[s * 2 + n] * (1.0 / stat[4 + s * 2 + n : 5 + s * 2 + n]) for n in range(2)]
        for parity in range(2):
            for p in range(4):
                ot_ref[parity, s * 4 + p] = halves[parity][:, p * 128 : (p + 1) * 128].astype(BF16)


def smem():
    return pl.BlockSpec(memory_space=pltpu.SMEM)


def params():
    return pltpu.CompilerParams(
        vmem_limit_bytes=VMEM_LIMIT, dimension_semantics=("arbitrary",)
    )


def wide_spec():
    return pl.BlockSpec((ROWS, 1024), lambda g: (0, g))


def full_forward(lengths, ctx, query, kv, early):
    return pl.pallas_call(
        full_forward_kernel,
        grid=(2,),
        in_specs=[
            smem(),
            smem(),
            wide_spec(),
            pl.BlockSpec((SEQ, 128), lambda g: (0, g)),
            pl.BlockSpec((SEQ, 128), lambda g: (0, 2 + g)),
            pl.BlockSpec(memory_space=pl.ANY),
            pl.BlockSpec(memory_space=pl.ANY),
        ],
        out_specs=[
            turned_spec(),
            pl.BlockSpec((1, 8, 512), lambda g: (g, 0, 0)),
        ],
        out_shape=[
            jax.ShapeDtypeStruct((2, 16, DH, ROWS), BF16),
            jax.ShapeDtypeStruct((2, 8, 512), F32),
        ],
        scratch_shapes=[pltpu.VMEM((4, DH, 512), F32), pltpu.VMEM((8, 512), F32)],
        compiler_params=params(),
        cost_estimate=pl.CostEstimate(flops=4 * H * ROWS * SEQ * DH * 4, bytes_accessed=3 << 20, transcendentals=H * ROWS * SEQ),
        name="full_forward",
    )(lengths, ctx, query, kv, kv, *early)


def full_backward_kernel(
    len_ref, ctx_ref, q_ref, k_ref, v_ref, o_ref, g_ref, lse_ref, early_a, early_b, early_c, early_d, dq_ref, dkv_ref, acc, corr, grads
):
    first_row = ctx_ref[0, 0] * ROWS
    rows = first_row + lax.broadcasted_iota(jnp.int32, (1, ROWS), 1)
    starts = row_starts(len_ref, rows)
    low = scalar_start(len_ref, first_row) // KB
    high = (first_row + ROWS + KB - 1) // KB
    acc[...] = jnp.zeros_like(acc)
    dkv_ref[...] = jnp.zeros_like(dkv_ref)
    for s in range(2):
        for p in range(4):
            at = slice(p * 128, (p + 1) * 128)
            halves = [g_ref[parity, s * 4 + p].astype(F32) for parity in range(2)]
            grads[s, at, :] = jnp.transpose(jnp.concatenate(halves, axis=0)).astype(BF16)
            for parity in range(2):
                product = halves[parity] * o_ref[parity, s * 4 + p].astype(F32)
                n = s * 2 + parity
                corr[n : n + 1, at] = jnp.sum(product, axis=0, keepdims=True)

    def block(b, carry):
        at = pl.ds(pl.multiple_of(b * KB, KB), KB)
        bias = mask_of(starts, rows, b * KB)
        keys, values = k_ref[at, :], v_ref[at, :]
        key_terms, value_terms = [], []
        for s in range(2):
            query, grad = stacked(q_ref, s, SCALE), grads[s]
            scores = nt(both_lanes(keys, s), query)
            grad_weights = nt(both_lanes(values, s), grad)
            turned = head_transposed(keys, s)
            low_weights, grad_scores = [], []
            for parity in range(2):
                n = s * 2 + parity
                half = slice(parity * KB, (parity + 1) * KB)
                weights = jnp.exp(scores[half] + bias - lse_ref[0, n : n + 1])
                low_weights.append(weights.astype(BF16))
                term = (weights * (grad_weights[half] - corr[n : n + 1])).astype(BF16)
                grad_scores.append(term)
                acc[n] += nn(turned, term)
            key_terms.append(nn(jnp.concatenate(grad_scores, axis=0), query))
            value_terms.append(nn(jnp.concatenate(low_weights, axis=0), grad))
        dkv_ref[0, at, :128] = head_pair(*key_terms).astype(BF16)
        dkv_ref[0, at, 128:] = head_pair(*value_terms).astype(BF16)
        return carry

    lax.fori_loop(low, high, block, 0)
    for s in range(2):
        store_rows(dq_ref, jnp.concatenate([acc[s * 2], acc[s * 2 + 1]], axis=0) * SCALE, s)


def turned_spec():
    return pl.BlockSpec((2, 8, DH, ROWS), lambda g: (0, g, 0, 0))


def full_backward(lengths, ctx, query, kv, out_t, grad_t, lse, early):
    return pl.pallas_call(
        full_backward_kernel,
        grid=(2,),
        in_specs=[
            smem(),
            smem(),
            wide_spec(),
            pl.BlockSpec((SEQ, 128), lambda g: (0, g)),
            pl.BlockSpec((SEQ, 128), lambda g: (0, 2 + g)),
            turned_spec(),
            turned_spec(),
            pl.BlockSpec((1, 8, 512), lambda g: (g, 0, 0)),
            pl.BlockSpec(memory_space=pl.ANY),
            pl.BlockSpec(memory_space=pl.ANY),
            pl.BlockSpec(memory_space=pl.ANY),
            pl.BlockSpec(memory_space=pl.ANY),
        ],
        out_specs=[wide_spec(), pl.BlockSpec((1, SEQ, 256), lambda g: (g, 0, 0))],
        out_shape=[
            jax.ShapeDtypeStruct((ROWS, H * DH), BF16),
            jax.ShapeDtypeStruct((2, SEQ, 256), BF16),
        ],
        scratch_shapes=[
            pltpu.VMEM((4, DH, 512), F32),
            pltpu.VMEM((8, 512), F32),
            pltpu.VMEM((2, 512, 128), BF16),
        ],
        compiler_params=params(),
        cost_estimate=pl.CostEstimate(
            flops=10 * H * ROWS * SEQ * DH * 4, bytes_accessed=5 << 20, transcendentals=H * ROWS * SEQ
        ),
        name="full_backward",
    )(lengths, ctx, query, kv, kv, out_t, grad_t, lse, *early)


def band_kernel(len_ref, ctx_ref, q_ref, k_ref, v_ref, g_ref, o_ref, dq_ref, dkv_ref):
    first_row = ctx_ref[0, 0] * ROWS
    rows = first_row + lax.broadcasted_iota(jnp.int32, (1, ROWS), 1)
    starts = jnp.maximum(row_starts(len_ref, rows), rows - (BAND - 1))
    bias = mask_of(starts, rows, first_row - BAND)
    keys, values = k_ref[...], v_ref[...]
    key_terms, value_terms = [], []
    for s in range(2):
        query, grad = stacked(q_ref, s, SCALE), stacked(g_ref, s)
        scores = nt(both_lanes(keys, s), query)
        turned = head_transposed(values, s)
        weights, low_weights, outs = [], [], []
        for parity in range(2):
            part = scores[parity * KB : (parity + 1) * KB] + bias
            grown = jnp.exp(part - jnp.max(part, axis=0, keepdims=True))
            grown = grown * (1.0 / jnp.sum(grown, axis=0, keepdims=True))
            weights.append(grown)
            low_weights.append(grown.astype(BF16))
            outs.append(nn(turned, low_weights[parity]))
        store_rows(o_ref, jnp.concatenate(outs, axis=0), s)
        corr = corrections(g_ref, o_ref, s)
        grad_weights = nt(both_lanes(values, s), grad)
        turned = head_transposed(keys, s)
        grad_scores, grad_query = [], []
        for parity in range(2):
            half = slice(parity * KB, (parity + 1) * KB)
            term = (weights[parity] * (grad_weights[half] - corr[parity])).astype(BF16)
            grad_scores.append(term)
            grad_query.append(nn(turned, term))
        store_rows(dq_ref, jnp.concatenate(grad_query, axis=0) * SCALE, s)
        key_terms.append(nn(jnp.concatenate(grad_scores, axis=0), query))
        value_terms.append(nn(jnp.concatenate(low_weights, axis=0), grad))
    dkv_ref[0, :, :128] = head_pair(*key_terms)
    dkv_ref[0, :, 128:] = head_pair(*value_terms)


def banded_layer(lengths, ctx, projected, kv_ext, grad):
    return pl.pallas_call(
        band_kernel,
        grid=(2,),
        in_specs=[
            smem(),
            smem(),
            wide_spec(),
            pl.BlockSpec((KB, 128), lambda g: (0, g)),
            pl.BlockSpec((KB, 128), lambda g: (0, 2 + g)),
            wide_spec(),
        ],
        out_specs=[wide_spec(), wide_spec(), pl.BlockSpec((1, KB, 256), lambda g: (g, 0, 0))],
        out_shape=[
            jax.ShapeDtypeStruct((ROWS, H * DH), BF16),
            jax.ShapeDtypeStruct((ROWS, H * DH), BF16),
            jax.ShapeDtypeStruct((2, KB, 256), F32),
        ],
        compiler_params=params(),
        cost_estimate=pl.CostEstimate(flops=14 * H * ROWS * KB * DH * 4, bytes_accessed=5 << 20, transcendentals=H * ROWS * KB),
        name="banded_layer",
    )(lengths, ctx, projected, kv_ext, kv_ext, grad)


def shifted(value, axis, count, step):
    return lax.ppermute(value, axis, [(i, (i + step) % count) for i in range(count)])


def swapped(value):
    return shifted(value, "c", 2, 1)


def steps_of(count):
    return sorted(range(1, count), key=lambda r: -min(r, count - r))


def sent_chunks(chunk, axis, count):
    me = lax.axis_index(axis)
    sends = [chunk(lax.rem(me + r, count)) for r in steps_of(count)]
    return sends, [shifted(send, axis, count, r) for send, r in zip(sends, steps_of(count))]


def summed(parts):
    total = parts[0].astype(F32)
    for part in parts[1:]:
        total = total + part.astype(F32)
    return total.astype(BF16)


def after(values, event):
    held, _ = lax.optimization_barrier((values, event))
    return held


def exchanged(value, axis, dim=0):
    return lax.all_to_all(value, axis, split_axis=dim, concat_axis=dim)


def gathered(value, axis, count):
    return exchanged(jnp.broadcast_to(value[None], (count, *value.shape)), axis)


def pick(array, index):
    return lax.dynamic_index_in_dim(array, index, 0, keepdims=False)


def first_gather(w_out, w_qkv):
    eighth = pick(w_out.reshape(8, 8, 1440), lax.axis_index(CTX))
    eighth = jnp.pad(eighth, ((0, 0), (0, 96))).reshape(96, 128)
    rows = pick(jnp.pad(w_qkv[:, CUT:], ((0, 3), (0, 0))).reshape(2, 24, 1536), lax.axis_index("xh"))
    rows = lax.dynamic_slice_in_dim(rows, lax.axis_index("y") * 384, 384, 1).reshape(72, 128)
    both = gathered(jnp.concatenate([eighth, rows], axis=0), "z", 8)
    return both[:, :96].reshape(8, 8, 1536), both[:, 96:].reshape(8, 24, 384)


def gathered_round_x(piece):
    me = lax.axis_index(X)
    whole = jnp.broadcast_to(piece[:, None, None], (8, 2, 2, 8, 1536))
    for r in steps_of(4):
        source = lax.rem(me - r + 4, 4)
        part = shifted(piece, X, 4, r).reshape(8, 1, 1, 8, 1536)
        whole = lax.dynamic_update_slice(whole, part, (0, lax.rem(source, 2), lax.div(source, 2), 0, 0))
    return whole


def sent_round(value, axis, count):
    return [shifted(value, axis, count, r) for r in steps_of(count)]


def placed_round_y(own, parts):
    me = lax.axis_index("y")
    whole = jnp.broadcast_to(own[:, :, :, None], (8, 2, 2, 4, 8, 1536))
    for r, part in zip(steps_of(4), parts):
        whole = lax.dynamic_update_index_in_dim(whole, part, lax.rem(me - r + 4, 4), 3)
    return whole.reshape(1024, 1536)


def per_device(query_a, key_a, value_a, resid_in, doc_lengths, w_out, w_qkv, grad_out, grad_resid):
    core = lax.axis_index("c")
    ctx = lax.axis_index(CTX).reshape(1, 1)
    lengths = doc_lengths
    w_b0 = lax.all_gather(jnp.pad(w_qkv[:, :CUT], ((0, 3), (0, 0))), FSDP, axis=0, tiled=True)
    out_piece, qkv_piece = first_gather(w_out, w_qkv)
    own_kv = after(jnp.concatenate([key_a[0], value_a[0]], axis=1), out_piece)
    kv = gathered(own_kv, CTX, 8).reshape(SEQ, 512)
    out_piece = gathered_round_x(out_piece)
    qkv_piece = gathered(qkv_piece, "y", 4).transpose(1, 2, 0, 3).reshape(8, 24, 1536)
    out_parts = sent_round(out_piece, "y", 4)
    spread = jnp.broadcast_to(qkv_piece[None], (4, 8, 24, 1536))
    query = query_a[0]
    attended_t, lse = full_forward(lengths, ctx, query, kv, [out_piece, spread])
    out_parts = after(out_parts, lse)
    own_o = placed_round_y(out_piece, out_parts)
    other_o = swapped(own_o)
    own_w = exchanged(spread, X).reshape(768, 1536)
    other_w = swapped(own_w)
    attended_t = attended_t.reshape(2, 1024, ROWS)
    own_t, other_t = pick(attended_t, core), pick(attended_t, 1 - core)
    pair_attended = jnp.concatenate([own_t, swapped(other_t)], axis=1)
    product = (tn(own_t, own_o) + tn(other_t, other_o))[:, :1440]
    resid_mid = (resid_in[0].astype(F32) + product).astype(BF16)
    resid_f = resid_mid.astype(F32)
    inverse_rms = lax.rsqrt(jnp.mean(resid_f * resid_f, axis=-1, keepdims=True) + EPSILON)
    normed = resid_f * inverse_rms
    normed_bf = normed.astype(BF16)
    turned = jnp.pad(normed_bf.T.reshape(32, 45, ROWS), ((0, 0), (0, 3), (0, 0)))
    padded = turned.reshape(1536, ROWS)
    turned = turned.reshape(8, 2, 2, 2, 24, ROWS).transpose(2, 3, 1, 0, 4, 5).reshape(2, 768, ROWS)
    own_n = pick(turned, core)
    sent_normed = pick(turned, 1 - core)
    pair_normed = jnp.concatenate([own_n, swapped(sent_normed)], axis=1)
    padded = after(padded, sent_normed)
    projected = jnp.concatenate(
        [tn(padded, w_b0).astype(BF16), (tn(own_n, own_w) + tn(sent_normed, other_w)).astype(BF16)],
        axis=1,
    )
    own_b = projected[:, H * DH :]
    tail = shifted(own_b, CTX, 8, 1)
    kv_ext = jnp.concatenate([tail, own_b], axis=0)
    banded, grad_qb, kv_grad = banded_layer(lengths, ctx, projected, kv_ext, grad_out[0])
    head = shifted(kv_grad[:, :BAND].astype(BF16), CTX, 8, -1).astype(F32)
    last = lax.axis_index(CTX) == 7
    own_grad = (kv_grad[:, BAND:] + jnp.where(last, 0.0, head)).astype(BF16)
    grad_proj = jnp.concatenate(
        [grad_qb, own_grad[0, :, :128], own_grad[1, :, :128], own_grad[0, :, 128:], own_grad[1, :, 128:]],
        axis=1,
    )
    pair_proj = jnp.concatenate([grad_proj, swapped(grad_proj)], axis=0)
    first = nn(pair_normed, pair_proj).astype(BF16).reshape(4, 192, 2560)
    first_sent = first
    first = exchanged(first, X)
    grad_turned = nt(w_b0, grad_proj[:, :CUT])
    own_gn, other_gn = nt(own_w, grad_proj[:, CUT:]), nt(other_w, grad_proj[:, CUT:])
    rest = jnp.stack([jnp.where(core == 0, own_gn, other_gn), jnp.where(core == 0, other_gn, own_gn)])
    rest = rest.reshape(2, 2, 2, 8, 24, ROWS).transpose(3, 2, 0, 1, 4, 5).reshape(32, 48, ROWS)
    grad_turned = (grad_turned.reshape(32, 48, ROWS) + rest)[:, :45].reshape(1440, ROWS)
    grad_normed = grad_turned.T
    middle = jnp.mean(grad_normed * normed, axis=-1, keepdims=True)
    grad_mid = (
        grad_resid[0].astype(F32) + inverse_rms * (grad_normed - normed * middle)
    ).astype(BF16)
    grad_mid = after(grad_mid, first_sent)
    wide_mid = jnp.pad(grad_mid, ((0, 0), (0, 96)))
    own_g, other_g = (nt(w, wide_mid).astype(BF16) for w in (own_o, other_o))
    grad_t = jnp.stack([jnp.where(core == 0, own_g, other_g), jnp.where(core == 0, other_g, own_g)])
    pair_mid = jnp.concatenate([wide_mid, swapped(wide_mid)], axis=0)
    def out_chunk(terms, i):
        return nn(terms, lax.dynamic_slice_in_dim(pair_mid, i * 384, 384, 1)).astype(BF16)

    sends, out_first = sent_chunks(lambda i: out_chunk(pair_attended, i), "y", 4)
    grad_t = after(grad_t, sends)
    grad_query, kv_terms = full_backward(
        lengths, ctx, query, kv, attended_t.reshape(2, 16, DH, ROWS), grad_t.reshape(2, 16, DH, ROWS), lse, [first_sent, *sends]
    )
    kv_terms = exchanged(kv_terms.reshape(2, 8, ROWS, 256), CTX, 1)
    first, out_first, pair_attended = after((first, out_first, pair_attended), grad_query)
    out_first.append(out_chunk(pair_attended, lax.axis_index("y")))
    first = summed(first).reshape(192, 4, 640).transpose(1, 0, 2)
    second = exchanged(first, "y")
    out_first = summed(out_first).reshape(8, 2, 2, 32, 384).transpose(2, 1, 0, 3, 4).reshape(4, 256, 384)
    _, out_second = sent_chunks(lambda i: pick(out_first, i), X, 4)
    out_second.append(pick(out_first, lax.axis_index(X)))
    own_terms = jnp.sum(kv_terms.astype(F32), axis=1).astype(BF16)
    grad_key = jnp.concatenate([own_terms[0, :, :128], own_terms[1, :, :128]], axis=1)
    grad_value = jnp.concatenate([own_terms[0, :, 128:], own_terms[1, :, 128:]], axis=1)
    both = jnp.concatenate(
        [summed(second).reshape(8, 120, 128), summed(out_second).reshape(8, 96, 128)], axis=1
    )
    both = exchanged(both, "z")
    both = jnp.sum(both.astype(F32), axis=0).astype(BF16)
    both = gathered(both, CTX, 8)
    grad_w_qkv = (
        both[:, :120].reshape(2, 4, 24, 640).transpose(0, 2, 1, 3).reshape(48, 2560)[:45].astype(F32)
    )
    grad_w_out = (
        both[:, 120:].reshape(2, 4, 32, 384).transpose(0, 2, 1, 3).reshape(64, 1536)[:, :1440].astype(F32)
    )
    return (
        banded[None],
        grad_mid[None],
        grad_query[None],
        grad_key[None],
        grad_value[None],
        grad_w_out,
        grad_w_qkv,
    )


def solution(mesh):
    torus = jax.sharding.Mesh(mesh.devices.reshape(2, 4, 8, 2, 2), ("xh", "y", "z", "xl", "c"))
    rows = P(FSDP, CTX, None)
    weight = P(FSDP, None)
    return jax.shard_map(
        per_device,
        mesh=torus,
        in_specs=(rows, rows, rows, rows, weight, weight, weight, rows, rows),
        out_specs=(rows, rows, rows, rows, rows, weight, weight),
        check_vma=False,
    )
```

```python
import functools

import jax
import jax.numpy as jnp
import numpy as np
from jax import lax
from jax.experimental import pallas as pl
from jax.experimental.pallas import tpu as pltpu
from jax.sharding import PartitionSpec as P

H = 32
KV = 4
DH = 64
BAND = 128
ROWS = 128
SEQ = 1024
KB = 256
MASKED = -1e30
LOWEST = -1e29
EPSILON = 1e-05
SCALE = DH**-0.5
CTX = ("xh", "y")
FSDP = ("z", "xl", "c")
X = ("xh", "xl")
F32 = jnp.float32
BF16 = jnp.bfloat16
CUT = 1024
VMEM_LIMIT = 48 * 1024 * 1024


def nt(a, b):
    return lax.dot_general(a, b, (((1,), (1,)), ((), ())), preferred_element_type=F32)


def nn(a, b):
    return lax.dot_general(a, b, (((1,), (0,)), ((), ())), preferred_element_type=F32)


def tn(a, b):
    return lax.dot_general(a, b, (((0,), (0,)), ((), ())), preferred_element_type=F32)


def row_starts(len_ref, rows):
    start, end = jnp.zeros_like(rows), 0
    for d in range(6):
        size = len_ref[0, d]
        end = end + size
        start = start + jnp.where(rows >= end, size, 0)
    return start


def scalar_start(len_ref, row):
    start, end = 0, 0
    for d in range(6):
        size = len_ref[0, d]
        end = end + size
        start = start + jnp.where(row >= end, size, 0)
    return start


def both_lanes(block, s):
    wide = block.astype(F32)
    lane = lax.broadcasted_iota(jnp.int32, wide.shape, 1)
    mine = jnp.where((lane < DH) if s == 0 else (lane >= DH), wide, 0.0)
    other = pltpu.roll(mine, DH, 1)
    pair = (mine, other) if s == 0 else (other, mine)
    return jnp.concatenate(pair, axis=0).astype(BF16)


def stacked(ref, s, scale=None):
    parts = [ref[:, s * 512 + p * 128 : s * 512 + (p + 1) * 128] for p in range(4)]
    whole = jnp.concatenate(parts, axis=0)
    if scale is not None:
        whole = whole * jnp.asarray(scale, whole.dtype)
    return whole


def head_transposed(block, s):
    return jnp.transpose(block.astype(F32))[s * DH : (s + 1) * DH].astype(BF16)


def mask_of(starts, rows, first_key):
    keys = first_key + lax.broadcasted_iota(jnp.int32, (KB, ROWS), 0)
    allowed = (keys >= starts) & (keys <= rows)
    bias = jnp.where(allowed, 0.0, MASKED)
    return jnp.concatenate([bias] * 4, axis=1)


def corrections(grad_ref, out_ref, s):
    even, odd = [], []
    for p in range(4):
        at = slice(s * 512 + p * 128, s * 512 + (p + 1) * 128)
        prod = jnp.transpose(grad_ref[:, at].astype(F32) * out_ref[:, at].astype(F32))
        even.append(jnp.sum(prod[:DH], axis=0, keepdims=True))
        odd.append(jnp.sum(prod[DH:], axis=0, keepdims=True))
    return jnp.concatenate(even, axis=1), jnp.concatenate(odd, axis=1)


def store_rows(ref, transposed, s):
    for p in range(4):
        at = slice(s * 512 + p * 128, s * 512 + (p + 1) * 128)
        ref[:, at] = jnp.transpose(transposed[:, p * 128 : (p + 1) * 128]).astype(ref.dtype)


def head_pair(first, second):
    lane = lax.broadcasted_iota(jnp.int32, (KB, 128), 1)
    low = first[:KB] + pltpu.roll(first[KB:], DH, 1)
    high = pltpu.roll(second[:KB], DH, 1) + second[KB:]
    return jnp.where(lane < DH, low, high)


def full_forward_kernel(
    len_ref, ctx_ref, q_ref, k_ref, v_ref, early_a, early_b, ot_ref, lse_ref, acc, stat
):
    first_row = ctx_ref[0, 0] * ROWS
    rows = first_row + lax.broadcasted_iota(jnp.int32, (1, ROWS), 1)
    starts = row_starts(len_ref, rows)
    low = scalar_start(len_ref, first_row) // KB
    high = (first_row + ROWS + KB - 1) // KB
    acc[...] = jnp.zeros_like(acc)
    stat[:4] = jnp.full((4, 512), LOWEST, F32)
    stat[4:] = jnp.zeros((4, 512), F32)

    def block(b, carry):
        at = pl.ds(pl.multiple_of(b * KB, KB), KB)
        bias = mask_of(starts, rows, b * KB)
        keys, values = k_ref[at, :], v_ref[at, :]
        for s in range(2):
            scores = nt(both_lanes(keys, s), stacked(q_ref, s, SCALE))
            turned = head_transposed(values, s)
            for parity in range(2):
                n = s * 2 + parity
                part = scores[parity * KB : (parity + 1) * KB] + bias
                old = stat[n : n + 1]
                new = jnp.maximum(old, jnp.max(part, axis=0, keepdims=True))
                weights = jnp.exp(part - new)
                fade = jnp.exp(old - new)
                stat[n : n + 1] = new
                stat[4 + n : 5 + n] = stat[4 + n : 5 + n] * fade + jnp.sum(weights, axis=0, keepdims=True)
                acc[n] = acc[n] * fade + nn(turned, weights.astype(BF16))
        return carry

    lax.fori_loop(low, high, block, 0)
    lse_ref[0] = jnp.concatenate([stat[:4] + jnp.log(stat[4:]), jnp.zeros((4, 512), F32)], axis=0)
    for s in range(2):
        halves = [acc[s * 2 + n] * (1.0 / stat[4 + s * 2 + n : 5 + s * 2 + n]) for n in range(2)]
        for parity in range(2):
            for p in range(4):
                ot_ref[parity, s * 4 + p] = halves[parity][:, p * 128 : (p + 1) * 128].astype(BF16)


def smem():
    return pl.BlockSpec(memory_space=pltpu.SMEM)


def params():
    return pltpu.CompilerParams(
        vmem_limit_bytes=VMEM_LIMIT, dimension_semantics=("arbitrary",)
    )


def wide_spec():
    return pl.BlockSpec((ROWS, 1024), lambda g: (0, g))


def full_forward(lengths, ctx, query, kv, early):
    return pl.pallas_call(
        full_forward_kernel,
        grid=(2,),
        in_specs=[
            smem(),
            smem(),
            wide_spec(),
            pl.BlockSpec((SEQ, 128), lambda g: (0, g)),
            pl.BlockSpec((SEQ, 128), lambda g: (0, 2 + g)),
            pl.BlockSpec(memory_space=pl.ANY),
            pl.BlockSpec(memory_space=pl.ANY),
        ],
        out_specs=[
            turned_spec(),
            pl.BlockSpec((1, 8, 512), lambda g: (g, 0, 0)),
        ],
        out_shape=[
            jax.ShapeDtypeStruct((2, 16, DH, ROWS), BF16),
            jax.ShapeDtypeStruct((2, 8, 512), F32),
        ],
        scratch_shapes=[pltpu.VMEM((4, DH, 512), F32), pltpu.VMEM((8, 512), F32)],
        compiler_params=params(),
        cost_estimate=pl.CostEstimate(flops=4 * H * ROWS * SEQ * DH * 4, bytes_accessed=3 << 20, transcendentals=H * ROWS * SEQ),
        name="full_forward",
    )(lengths, ctx, query, kv, kv, *early)


def full_backward_kernel(
    len_ref, ctx_ref, q_ref, k_ref, v_ref, o_ref, g_ref, lse_ref, early_a, early_b, early_c, early_d, dq_ref, dkv_ref, acc, corr, grads
):
    first_row = ctx_ref[0, 0] * ROWS
    rows = first_row + lax.broadcasted_iota(jnp.int32, (1, ROWS), 1)
    starts = row_starts(len_ref, rows)
    low = scalar_start(len_ref, first_row) // KB
    high = (first_row + ROWS + KB - 1) // KB
    acc[...] = jnp.zeros_like(acc)
    dkv_ref[...] = jnp.zeros_like(dkv_ref)
    for s in range(2):
        for p in range(4):
            at = slice(p * 128, (p + 1) * 128)
            halves = [g_ref[parity, s * 4 + p].astype(F32) for parity in range(2)]
            grads[s, at, :] = jnp.transpose(jnp.concatenate(halves, axis=0)).astype(BF16)
            for parity in range(2):
                product = halves[parity] * o_ref[parity, s * 4 + p].astype(F32)
                n = s * 2 + parity
                corr[n : n + 1, at] = jnp.sum(product, axis=0, keepdims=True)

    def block(b, carry):
        at = pl.ds(pl.multiple_of(b * KB, KB), KB)
        bias = mask_of(starts, rows, b * KB)
        keys, values = k_ref[at, :], v_ref[at, :]
        key_terms, value_terms = [], []
        for s in range(2):
            query, grad = stacked(q_ref, s, SCALE), grads[s]
            scores = nt(both_lanes(keys, s), query)
            grad_weights = nt(both_lanes(values, s), grad)
            turned = head_transposed(keys, s)
            low_weights, grad_scores = [], []
            for parity in range(2):
                n = s * 2 + parity
                half = slice(parity * KB, (parity + 1) * KB)
                weights = jnp.exp(scores[half] + bias - lse_ref[0, n : n + 1])
                low_weights.append(weights.astype(BF16))
                term = (weights * (grad_weights[half] - corr[n : n + 1])).astype(BF16)
                grad_scores.append(term)
                acc[n] += nn(turned, term)
            key_terms.append(nn(jnp.concatenate(grad_scores, axis=0), query))
            value_terms.append(nn(jnp.concatenate(low_weights, axis=0), grad))
        dkv_ref[0, at, :128] = head_pair(*key_terms).astype(BF16)
        dkv_ref[0, at, 128:] = head_pair(*value_terms).astype(BF16)
        return carry

    lax.fori_loop(low, high, block, 0)
    for s in range(2):
        store_rows(dq_ref, jnp.concatenate([acc[s * 2], acc[s * 2 + 1]], axis=0) * SCALE, s)


def turned_spec():
    return pl.BlockSpec((2, 8, DH, ROWS), lambda g: (0, g, 0, 0))


def full_backward(lengths, ctx, query, kv, out_t, grad_t, lse, early):
    return pl.pallas_call(
        full_backward_kernel,
        grid=(2,),
        in_specs=[
            smem(),
            smem(),
            wide_spec(),
            pl.BlockSpec((SEQ, 128), lambda g: (0, g)),
            pl.BlockSpec((SEQ, 128), lambda g: (0, 2 + g)),
            turned_spec(),
            turned_spec(),
            pl.BlockSpec((1, 8, 512), lambda g: (g, 0, 0)),
            pl.BlockSpec(memory_space=pl.ANY),
            pl.BlockSpec(memory_space=pl.ANY),
            pl.BlockSpec(memory_space=pl.ANY),
            pl.BlockSpec(memory_space=pl.ANY),
        ],
        out_specs=[wide_spec(), pl.BlockSpec((1, SEQ, 256), lambda g: (g, 0, 0))],
        out_shape=[
            jax.ShapeDtypeStruct((ROWS, H * DH), BF16),
            jax.ShapeDtypeStruct((2, SEQ, 256), BF16),
        ],
        scratch_shapes=[
            pltpu.VMEM((4, DH, 512), F32),
            pltpu.VMEM((8, 512), F32),
            pltpu.VMEM((2, 512, 128), BF16),
        ],
        compiler_params=params(),
        cost_estimate=pl.CostEstimate(
            flops=10 * H * ROWS * SEQ * DH * 4, bytes_accessed=5 << 20, transcendentals=H * ROWS * SEQ
        ),
        name="full_backward",
    )(lengths, ctx, query, kv, kv, out_t, grad_t, lse, *early)


def band_kernel(len_ref, ctx_ref, q_ref, k_ref, v_ref, g_ref, o_ref, dq_ref, dkv_ref):
    first_row = ctx_ref[0, 0] * ROWS
    rows = first_row + lax.broadcasted_iota(jnp.int32, (1, ROWS), 1)
    starts = jnp.maximum(row_starts(len_ref, rows), rows - (BAND - 1))
    bias = mask_of(starts, rows, first_row - BAND)
    keys, values = k_ref[...], v_ref[...]
    key_terms, value_terms = [], []
    for s in range(2):
        query, grad = stacked(q_ref, s, SCALE), stacked(g_ref, s)
        scores = nt(both_lanes(keys, s), query)
        turned = head_transposed(values, s)
        weights, low_weights, outs = [], [], []
        for parity in range(2):
            part = scores[parity * KB : (parity + 1) * KB] + bias
            grown = jnp.exp(part - jnp.max(part, axis=0, keepdims=True))
            grown = grown * (1.0 / jnp.sum(grown, axis=0, keepdims=True))
            weights.append(grown)
            low_weights.append(grown.astype(BF16))
            outs.append(nn(turned, low_weights[parity]))
        store_rows(o_ref, jnp.concatenate(outs, axis=0), s)
        corr = corrections(g_ref, o_ref, s)
        grad_weights = nt(both_lanes(values, s), grad)
        turned = head_transposed(keys, s)
        grad_scores, grad_query = [], []
        for parity in range(2):
            half = slice(parity * KB, (parity + 1) * KB)
            term = (weights[parity] * (grad_weights[half] - corr[parity])).astype(BF16)
            grad_scores.append(term)
            grad_query.append(nn(turned, term))
        store_rows(dq_ref, jnp.concatenate(grad_query, axis=0) * SCALE, s)
        key_terms.append(nn(jnp.concatenate(grad_scores, axis=0), query))
        value_terms.append(nn(jnp.concatenate(low_weights, axis=0), grad))
    dkv_ref[0, :, :128] = head_pair(*key_terms)
    dkv_ref[0, :, 128:] = head_pair(*value_terms)


def banded_layer(lengths, ctx, projected, kv_ext, grad):
    return pl.pallas_call(
        band_kernel,
        grid=(2,),
        in_specs=[
            smem(),
            smem(),
            wide_spec(),
            pl.BlockSpec((KB, 128), lambda g: (0, g)),
            pl.BlockSpec((KB, 128), lambda g: (0, 2 + g)),
            wide_spec(),
        ],
        out_specs=[wide_spec(), wide_spec(), pl.BlockSpec((1, KB, 256), lambda g: (g, 0, 0))],
        out_shape=[
            jax.ShapeDtypeStruct((ROWS, H * DH), BF16),
            jax.ShapeDtypeStruct((ROWS, H * DH), BF16),
            jax.ShapeDtypeStruct((2, KB, 256), F32),
        ],
        compiler_params=params(),
        cost_estimate=pl.CostEstimate(flops=14 * H * ROWS * KB * DH * 4, bytes_accessed=5 << 20, transcendentals=H * ROWS * KB),
        name="banded_layer",
    )(lengths, ctx, projected, kv_ext, kv_ext, grad)


def shifted(value, axis, count, step):
    return lax.ppermute(value, axis, [(i, (i + step) % count) for i in range(count)])


def swapped(value):
    return shifted(value, "c", 2, 1)


def steps_of(count):
    return sorted(range(1, count), key=lambda r: -min(r, count - r))


def sent_chunks(chunk, axis, count):
    me = lax.axis_index(axis)
    sends = [chunk(lax.rem(me + r, count)) for r in steps_of(count)]
    return sends, [shifted(send, axis, count, r) for send, r in zip(sends, steps_of(count))]


def summed(parts):
    total = parts[0].astype(F32)
    for part in parts[1:]:
        total = total + part.astype(F32)
    return total.astype(BF16)


def after(values, event):
    held, _ = lax.optimization_barrier((values, event))
    return held


def sum_by_rows_kernel(a_ref, b_ref, c_ref, d_ref, early, o_ref):
    for block in range(32):
        z, xl, xh = block // 4, block // 2 % 2, block % 2
        at = slice(block * 32, (block + 1) * 32)
        total = (a_ref[at, :].astype(F32) + b_ref[at, :].astype(F32)) + (
            c_ref[at, :].astype(F32) + d_ref[at, :].astype(F32)
        )
        o_ref[xh * 2 + xl, z] = total.astype(BF16)


def sum_by_rows(parts, early):
    vmem = pl.BlockSpec(memory_space=pltpu.VMEM)
    return pl.pallas_call(
        sum_by_rows_kernel,
        in_specs=[vmem] * 4 + [pl.BlockSpec(memory_space=pl.ANY)],
        out_specs=vmem,
        out_shape=jax.ShapeDtypeStruct((4, 8, 32, 384), BF16),
        compiler_params=pltpu.CompilerParams(vmem_limit_bytes=VMEM_LIMIT),
        cost_estimate=pl.CostEstimate(flops=1 << 21, bytes_accessed=4 << 20, transcendentals=0),
        name="sum_by_rows",
    )(*parts, early)


def sum_by_columns_kernel(p_ref, early, o_ref):
    for y in range(4):
        at = slice(y * 640, (y + 1) * 640)
        total = (p_ref[0, :, at].astype(F32) + p_ref[1, :, at].astype(F32)) + (
            p_ref[2, :, at].astype(F32) + p_ref[3, :, at].astype(F32)
        )
        o_ref[y] = total.astype(BF16)


def sum_by_columns(parts, early):
    vmem = pl.BlockSpec(memory_space=pltpu.VMEM)
    return pl.pallas_call(
        sum_by_columns_kernel,
        in_specs=[vmem, pl.BlockSpec(memory_space=pl.ANY)],
        out_specs=vmem,
        out_shape=jax.ShapeDtypeStruct((4, 192, 640), BF16),
        compiler_params=pltpu.CompilerParams(vmem_limit_bytes=VMEM_LIMIT),
        cost_estimate=pl.CostEstimate(flops=1 << 21, bytes_accessed=5 << 20, transcendentals=0),
        name="sum_by_columns",
    )(parts, early)


def exchanged(value, axis, dim=0):
    return lax.all_to_all(value, axis, split_axis=dim, concat_axis=dim)


def gathered(value, axis, count):
    return exchanged(jnp.broadcast_to(value[None], (count, *value.shape)), axis)


def pick(array, index):
    return lax.dynamic_index_in_dim(array, index, 0, keepdims=False)


def first_gather(w_out, w_qkv):
    eighth = pick(w_out.reshape(8, 8, 1440), lax.axis_index(CTX))
    eighth = column_groups(jnp.pad(eighth, ((0, 0), (0, 96))))
    rows = pick(jnp.pad(w_qkv[:, CUT:], ((0, 3), (0, 0))).reshape(2, 24, 1536), lax.axis_index("xh"))
    rows = column_groups(lax.dynamic_slice_in_dim(rows, lax.axis_index("y") * 384, 384, 1))
    both = gathered(jnp.concatenate([eighth, rows], axis=0), "z", 8)
    return from_column_groups(both[:, :96], 8), from_column_groups(both[:, 96:], 24)


def gathered_round_x(piece):
    me = lax.axis_index(X)
    whole = jnp.broadcast_to(piece[:, None, None], (8, 2, 2, 8, 1536))
    for r in steps_of(4):
        source = lax.rem(me - r + 4, 4)
        part = shifted(piece, X, 4, r).reshape(8, 1, 1, 8, 1536)
        whole = lax.dynamic_update_slice(whole, part, (0, lax.rem(source, 2), lax.div(source, 2), 0, 0))
    return whole


def sent_round(value, axis, count):
    return [shifted(value, axis, count, r) for r in steps_of(count)]


def ring_sources(axis, count):
    me = lax.axis_index(axis)
    return [me] + [lax.rem(me - r + count, count) for r in steps_of(count)]


def weighted(terms, parts, sources):
    total = None
    for mine, theirs in zip(terms, parts):
        for part, source in zip(theirs, sources):
            product = tn(pick(mine, source), part)
            total = product if total is None else total + product
    return total


def back_through(grad, parts, sources, dtype):
    count, depth = len(parts), parts[0].shape[0]
    whole = jnp.zeros((count, depth, ROWS), dtype)
    for part, source in zip(parts, sources):
        whole = lax.dynamic_update_index_in_dim(whole, nt(part, grad).astype(dtype), source, 0)
    return whole


def column_groups(rows):
    *lead, r, width = rows.shape
    n = width // 128
    return jnp.swapaxes(rows.reshape(*lead, r, n, 128), -3, -2).reshape(*lead, n * r, 128)


def from_column_groups(groups, r):
    *lead, size, _ = groups.shape
    n = size // r
    return jnp.swapaxes(groups.reshape(*lead, n, r, 128), -3, -2).reshape(*lead, r, n * 128)


def per_device(query_a, key_a, value_a, resid_in, doc_lengths, w_out, w_qkv, grad_out, grad_resid):
    core = lax.axis_index("c")
    ctx = lax.axis_index(CTX).reshape(1, 1)
    lengths = doc_lengths
    w_b0 = lax.all_gather(jnp.pad(w_qkv[:, :CUT], ((0, 3), (0, 0))), FSDP, axis=0, tiled=True)
    out_piece, qkv_piece = first_gather(w_out, w_qkv)
    own_kv = after(jnp.concatenate([key_a[0], value_a[0]], axis=1), out_piece)
    kv = gathered(own_kv, CTX, 8).reshape(SEQ, 512)
    out_piece = gathered_round_x(out_piece)
    qkv_piece = gathered(qkv_piece, "y", 4).transpose(1, 2, 0, 3).reshape(8, 24, 1536)
    out_parts = sent_round(out_piece, "y", 4)
    qkv_parts = sent_round(qkv_piece, X, 4)
    query = query_a[0]
    attended_t, lse = full_forward(lengths, ctx, query, kv, [out_piece, qkv_piece])
    own_o = [part.reshape(256, 1536) for part in [out_piece, *out_parts]]
    other_o = [swapped(part) for part in own_o]
    own_w = [part.reshape(192, 1536) for part in [qkv_piece, *qkv_parts]]
    other_w = [swapped(part) for part in own_w]
    y_sources, x_sources = ring_sources("y", 4), ring_sources(X, 4)
    attended_t = attended_t.reshape(2, 1024, ROWS)
    own_t, other_t = pick(attended_t, core), pick(attended_t, 1 - core)
    pair_attended = jnp.concatenate([own_t, swapped(other_t)], axis=1)
    by_y = attended_t.reshape(2, 8, 2, 2, 4, 8, ROWS).transpose(0, 4, 1, 2, 3, 5, 6).reshape(2, 4, 256, ROWS)
    terms = (pick(by_y, core), pick(by_y, 1 - core))
    product = weighted(terms, (own_o, other_o), y_sources)[:, :1440]
    resid_mid = (resid_in[0].astype(F32) + product).astype(BF16)
    resid_f = resid_mid.astype(F32)
    inverse_rms = lax.rsqrt(jnp.mean(resid_f * resid_f, axis=-1, keepdims=True) + EPSILON)
    normed = resid_f * inverse_rms
    normed_bf = normed.astype(BF16)
    turned = jnp.pad(normed_bf.T.reshape(32, 45, ROWS), ((0, 0), (0, 3), (0, 0)))
    padded = turned.reshape(1536, ROWS)
    turned = turned.reshape(8, 2, 2, 2, 24, ROWS).transpose(2, 3, 1, 0, 4, 5).reshape(2, 768, ROWS)
    own_n = pick(turned, core)
    sent_normed = pick(turned, 1 - core)
    pair_normed = jnp.concatenate([own_n, swapped(sent_normed)], axis=1)
    padded = after(padded, sent_normed)
    projected = jnp.concatenate(
        [
            tn(padded, w_b0).astype(BF16),
            weighted(
                (own_n.reshape(4, 192, ROWS), sent_normed.reshape(4, 192, ROWS)), (own_w, other_w), x_sources
            ).astype(BF16),
        ],
        axis=1,
    )
    own_b = projected[:, H * DH :]
    tail = shifted(own_b, CTX, 8, 1)
    kv_ext = jnp.concatenate([tail, own_b], axis=0)
    banded, grad_qb, kv_grad = banded_layer(lengths, ctx, projected, kv_ext, grad_out[0])
    head = shifted(kv_grad[:, :BAND].astype(BF16), CTX, 8, -1).astype(F32)
    last = lax.axis_index(CTX) == 7
    own_grad = (kv_grad[:, BAND:] + jnp.where(last, 0.0, head)).astype(BF16)
    grad_proj = jnp.concatenate(
        [grad_qb, own_grad[0, :, :128], own_grad[1, :, :128], own_grad[0, :, 128:], own_grad[1, :, 128:]],
        axis=1,
    )
    pair_proj = jnp.concatenate([grad_proj, swapped(grad_proj)], axis=0)
    first = nn(pair_normed, pair_proj).astype(BF16).reshape(4, 192, 2560)
    first_sent = first
    first = exchanged(first, X)
    grad_turned = nt(w_b0, grad_proj[:, :CUT])
    own_gn, other_gn = (
        back_through(grad_proj[:, CUT:], parts, x_sources, F32) for parts in (own_w, other_w)
    )
    rest = jnp.stack([jnp.where(core == 0, own_gn, other_gn), jnp.where(core == 0, other_gn, own_gn)])
    rest = rest.reshape(2, 2, 2, 8, 24, ROWS).transpose(3, 2, 0, 1, 4, 5).reshape(32, 48, ROWS)
    grad_turned = (grad_turned.reshape(32, 48, ROWS) + rest)[:, :45].reshape(1440, ROWS)
    grad_normed = grad_turned.T
    middle = jnp.mean(grad_normed * normed, axis=-1, keepdims=True)
    grad_mid = (
        grad_resid[0].astype(F32) + inverse_rms * (grad_normed - normed * middle)
    ).astype(BF16)
    grad_mid = after(grad_mid, first_sent)
    wide_mid = jnp.pad(grad_mid, ((0, 0), (0, 96)))
    own_g, other_g = (back_through(wide_mid, parts, y_sources, BF16) for parts in (own_o, other_o))
    grad_t = jnp.stack([jnp.where(core == 0, own_g, other_g), jnp.where(core == 0, other_g, own_g)])
    pair_mid = jnp.concatenate([wide_mid, swapped(wide_mid)], axis=0)
    def out_chunk(terms, i):
        return nn(terms, lax.dynamic_slice_in_dim(pair_mid, i * 384, 384, 1)).astype(BF16)

    grad_t = grad_t.reshape(2, 4, 8, 2, 2, 8, ROWS).transpose(0, 2, 3, 4, 1, 5, 6)
    sends, out_first = sent_chunks(lambda i: out_chunk(pair_attended, i), "y", 4)
    grad_t = after(grad_t, sends)
    grad_query, kv_terms = full_backward(
        lengths, ctx, query, kv, attended_t.reshape(2, 16, DH, ROWS), grad_t.reshape(2, 16, DH, ROWS), lse, [first_sent, *sends]
    )
    kv_terms = exchanged(kv_terms.reshape(2, 8, ROWS, 256), CTX, 1)
    pair_attended = after(pair_attended, grad_query)
    out_first.append(out_chunk(pair_attended, lax.axis_index("y")))
    out_first = sum_by_rows(out_first, kv_terms)
    first = sum_by_columns(first, kv_terms)
    second = exchanged(first, "y")
    _, out_second = sent_chunks(lambda i: pick(out_first, i).reshape(256, 384), X, 4)
    out_second.append(pick(out_first, lax.axis_index(X)).reshape(256, 384))
    own_terms = jnp.sum(kv_terms.astype(F32), axis=1).astype(BF16)
    grad_key = jnp.concatenate([own_terms[0, :, :128], own_terms[1, :, :128]], axis=1)
    grad_value = jnp.concatenate([own_terms[0, :, 128:], own_terms[1, :, 128:]], axis=1)
    both = jnp.concatenate(
        [
            column_groups(summed(second).reshape(8, 24, 640)),
            column_groups(summed(out_second).reshape(8, 32, 384)),
        ],
        axis=1,
    )
    both = exchanged(both, "z")
    both = jnp.sum(both.astype(F32), axis=0).astype(BF16)
    both = gathered(both, CTX, 8)
    qkv_rows = from_column_groups(both[:, :120], 24).reshape(2, 4, 24, 640)
    grad_w_qkv = qkv_rows.transpose(0, 2, 1, 3).reshape(48, 2560)[:45].astype(F32)
    out_rows = from_column_groups(both[:, 120:], 32).reshape(2, 4, 32, 384)
    grad_w_out = out_rows.transpose(0, 2, 1, 3).reshape(64, 1536)[:, :1440].astype(F32)
    return (
        banded[None],
        grad_mid[None],
        grad_query[None],
        grad_key[None],
        grad_value[None],
        grad_w_out,
        grad_w_qkv,
    )


def solution(mesh):
    torus = jax.sharding.Mesh(mesh.devices.reshape(2, 4, 8, 2, 2), ("xh", "y", "z", "xl", "c"))
    rows = P(FSDP, CTX, None)
    weight = P(FSDP, None)
    return jax.shard_map(
        per_device,
        mesh=torus,
        in_specs=(rows, rows, rows, rows, weight, weight, weight, rows, rows),
        out_specs=(rows, rows, rows, rows, rows, weight, weight),
        check_vma=False,
    )
```

```python
import functools

import jax
import jax.numpy as jnp
import numpy as np
from jax import lax
from jax.experimental import pallas as pl
from jax.experimental.pallas import tpu as pltpu
from jax.sharding import PartitionSpec as P

H = 32
KV = 4
DH = 64
BAND = 128
ROWS = 128
SEQ = 1024
KB = 256
MASKED = -1e30
LOWEST = -1e29
EPSILON = 1e-05
SCALE = DH**-0.5
CTX = ("xh", "y")
FSDP = ("z", "xl", "c")
X = ("xh", "xl")
F32 = jnp.float32
BF16 = jnp.bfloat16
CUT = 1024
VMEM_LIMIT = 48 * 1024 * 1024


def nt(a, b):
    return lax.dot_general(a, b, (((1,), (1,)), ((), ())), preferred_element_type=F32)


def nn(a, b):
    return lax.dot_general(a, b, (((1,), (0,)), ((), ())), preferred_element_type=F32)


def tn(a, b):
    return lax.dot_general(a, b, (((0,), (0,)), ((), ())), preferred_element_type=F32)


def row_starts(len_ref, rows):
    start, end = jnp.zeros_like(rows), 0
    for d in range(6):
        size = len_ref[0, d]
        end = end + size
        start = start + jnp.where(rows >= end, size, 0)
    return start


def scalar_start(len_ref, row):
    start, end = 0, 0
    for d in range(6):
        size = len_ref[0, d]
        end = end + size
        start = start + jnp.where(row >= end, size, 0)
    return start


def both_lanes(block, s):
    wide = block.astype(F32)
    lane = lax.broadcasted_iota(jnp.int32, wide.shape, 1)
    mine = jnp.where((lane < DH) if s == 0 else (lane >= DH), wide, 0.0)
    other = pltpu.roll(mine, DH, 1)
    pair = (mine, other) if s == 0 else (other, mine)
    return jnp.concatenate(pair, axis=0).astype(BF16)


def stacked(ref, s, scale=None):
    parts = [ref[:, s * 512 + p * 128 : s * 512 + (p + 1) * 128] for p in range(4)]
    whole = jnp.concatenate(parts, axis=0)
    if scale is not None:
        whole = whole * jnp.asarray(scale, whole.dtype)
    return whole


def head_transposed(block, s):
    return jnp.transpose(block.astype(F32))[s * DH : (s + 1) * DH].astype(BF16)


def mask_of(starts, rows, first_key):
    keys = first_key + lax.broadcasted_iota(jnp.int32, (KB, ROWS), 0)
    allowed = (keys >= starts) & (keys <= rows)
    bias = jnp.where(allowed, 0.0, MASKED)
    return jnp.concatenate([bias] * 4, axis=1)


def corrections(grad_ref, out_ref, s):
    even, odd = [], []
    for p in range(4):
        at = slice(s * 512 + p * 128, s * 512 + (p + 1) * 128)
        prod = jnp.transpose(grad_ref[:, at].astype(F32) * out_ref[:, at].astype(F32))
        even.append(jnp.sum(prod[:DH], axis=0, keepdims=True))
        odd.append(jnp.sum(prod[DH:], axis=0, keepdims=True))
    return jnp.concatenate(even, axis=1), jnp.concatenate(odd, axis=1)


def store_rows(ref, transposed, s):
    for p in range(4):
        at = slice(s * 512 + p * 128, s * 512 + (p + 1) * 128)
        ref[:, at] = jnp.transpose(transposed[:, p * 128 : (p + 1) * 128]).astype(ref.dtype)


def head_pair(first, second):
    lane = lax.broadcasted_iota(jnp.int32, (KB, 128), 1)
    low = first[:KB] + pltpu.roll(first[KB:], DH, 1)
    high = pltpu.roll(second[:KB], DH, 1) + second[KB:]
    return jnp.where(lane < DH, low, high)


def full_forward_kernel(
    len_ref, ctx_ref, q_ref, k_ref, v_ref, ot_ref, lse_ref, acc, stat
):
    first_row = ctx_ref[0, 0] * ROWS
    rows = first_row + lax.broadcasted_iota(jnp.int32, (1, ROWS), 1)
    starts = row_starts(len_ref, rows)
    low = scalar_start(len_ref, first_row) // KB
    high = (first_row + ROWS + KB - 1) // KB
    acc[...] = jnp.zeros_like(acc)
    stat[:4] = jnp.full((4, 512), LOWEST, F32)
    stat[4:] = jnp.zeros((4, 512), F32)

    def block(b, carry):
        at = pl.ds(pl.multiple_of(b * KB, KB), KB)
        bias = mask_of(starts, rows, b * KB)
        keys, values = k_ref[at, :], v_ref[at, :]
        for s in range(2):
            scores = nt(both_lanes(keys, s), stacked(q_ref, s, SCALE))
            turned = head_transposed(values, s)
            for parity in range(2):
                n = s * 2 + parity
                part = scores[parity * KB : (parity + 1) * KB] + bias
                old = stat[n : n + 1]
                new = jnp.maximum(old, jnp.max(part, axis=0, keepdims=True))
                weights = jnp.exp(part - new)
                fade = jnp.exp(old - new)
                stat[n : n + 1] = new
                stat[4 + n : 5 + n] = stat[4 + n : 5 + n] * fade + jnp.sum(weights, axis=0, keepdims=True)
                acc[n] = acc[n] * fade + nn(turned, weights.astype(BF16))
        return carry

    lax.fori_loop(low, high, block, 0)
    lse_ref[0] = jnp.concatenate([stat[:4] + jnp.log(stat[4:]), jnp.zeros((4, 512), F32)], axis=0)
    for s in range(2):
        halves = [acc[s * 2 + n] * (1.0 / stat[4 + s * 2 + n : 5 + s * 2 + n]) for n in range(2)]
        for parity in range(2):
            for p in range(4):
                ot_ref[parity, s * 4 + p] = halves[parity][:, p * 128 : (p + 1) * 128].astype(BF16)


def smem():
    return pl.BlockSpec(memory_space=pltpu.SMEM)


def params():
    return pltpu.CompilerParams(
        vmem_limit_bytes=VMEM_LIMIT, dimension_semantics=("arbitrary",)
    )


def wide_spec():
    return pl.BlockSpec((ROWS, 1024), lambda g: (0, g))


def full_forward(lengths, ctx, query, kv):
    return pl.pallas_call(
        full_forward_kernel,
        grid=(2,),
        in_specs=[
            smem(),
            smem(),
            wide_spec(),
            pl.BlockSpec((SEQ, 128), lambda g: (0, g)),
            pl.BlockSpec((SEQ, 128), lambda g: (0, 2 + g)),
        ],
        out_specs=[
            turned_spec(),
            pl.BlockSpec((1, 8, 512), lambda g: (g, 0, 0)),
        ],
        out_shape=[
            jax.ShapeDtypeStruct((2, 16, DH, ROWS), BF16),
            jax.ShapeDtypeStruct((2, 8, 512), F32),
        ],
        scratch_shapes=[pltpu.VMEM((4, DH, 512), F32), pltpu.VMEM((8, 512), F32)],
        compiler_params=params(),
        cost_estimate=pl.CostEstimate(flops=4 * H * ROWS * SEQ * DH * 4, bytes_accessed=3 << 20, transcendentals=H * ROWS * SEQ),
        name="full_forward",
    )(lengths, ctx, query, kv, kv)


def full_backward_kernel(
    len_ref, ctx_ref, q_ref, k_ref, v_ref, o_ref, g_ref, lse_ref, early_a, early_b, dq_ref, dkv_ref, acc, corr, grads
):
    first_row = ctx_ref[0, 0] * ROWS
    rows = first_row + lax.broadcasted_iota(jnp.int32, (1, ROWS), 1)
    starts = row_starts(len_ref, rows)
    low = scalar_start(len_ref, first_row) // KB
    high = (first_row + ROWS + KB - 1) // KB
    acc[...] = jnp.zeros_like(acc)
    dkv_ref[...] = jnp.zeros_like(dkv_ref)
    for s in range(2):
        for p in range(4):
            at = slice(p * 128, (p + 1) * 128)
            halves = [g_ref[parity, s * 4 + p].astype(F32) for parity in range(2)]
            grads[s, at, :] = jnp.transpose(jnp.concatenate(halves, axis=0)).astype(BF16)
            for parity in range(2):
                product = halves[parity] * o_ref[parity, s * 4 + p].astype(F32)
                n = s * 2 + parity
                corr[n : n + 1, at] = jnp.sum(product, axis=0, keepdims=True)

    def block(b, carry):
        at = pl.ds(pl.multiple_of(b * KB, KB), KB)
        bias = mask_of(starts, rows, b * KB)
        keys, values = k_ref[at, :], v_ref[at, :]
        key_terms, value_terms = [], []
        for s in range(2):
            query, grad = stacked(q_ref, s, SCALE), grads[s]
            scores = nt(both_lanes(keys, s), query)
            grad_weights = nt(both_lanes(values, s), grad)
            turned = head_transposed(keys, s)
            low_weights, grad_scores = [], []
            for parity in range(2):
                n = s * 2 + parity
                half = slice(parity * KB, (parity + 1) * KB)
                weights = jnp.exp(scores[half] + bias - lse_ref[0, n : n + 1])
                low_weights.append(weights.astype(BF16))
                term = (weights * (grad_weights[half] - corr[n : n + 1])).astype(BF16)
                grad_scores.append(term)
                acc[n] += nn(turned, term)
            key_terms.append(nn(jnp.concatenate(grad_scores, axis=0), query))
            value_terms.append(nn(jnp.concatenate(low_weights, axis=0), grad))
        dkv_ref[0, at, :128] = head_pair(*key_terms).astype(BF16)
        dkv_ref[0, at, 128:] = head_pair(*value_terms).astype(BF16)
        return carry

    lax.fori_loop(low, high, block, 0)
    for s in range(2):
        store_rows(dq_ref, jnp.concatenate([acc[s * 2], acc[s * 2 + 1]], axis=0) * SCALE, s)


def turned_spec():
    return pl.BlockSpec((2, 8, DH, ROWS), lambda g: (0, g, 0, 0))


def full_backward(lengths, ctx, query, kv, out_t, grad_t, lse, early):
    return pl.pallas_call(
        full_backward_kernel,
        grid=(2,),
        in_specs=[
            smem(),
            smem(),
            wide_spec(),
            pl.BlockSpec((SEQ, 128), lambda g: (0, g)),
            pl.BlockSpec((SEQ, 128), lambda g: (0, 2 + g)),
            turned_spec(),
            turned_spec(),
            pl.BlockSpec((1, 8, 512), lambda g: (g, 0, 0)),
            pl.BlockSpec(memory_space=pl.ANY),
            pl.BlockSpec(memory_space=pl.ANY),
        ],
        out_specs=[wide_spec(), pl.BlockSpec((1, SEQ, 256), lambda g: (g, 0, 0))],
        out_shape=[
            jax.ShapeDtypeStruct((ROWS, H * DH), BF16),
            jax.ShapeDtypeStruct((2, SEQ, 256), BF16),
        ],
        scratch_shapes=[
            pltpu.VMEM((4, DH, 512), F32),
            pltpu.VMEM((8, 512), F32),
            pltpu.VMEM((2, 512, 128), BF16),
        ],
        compiler_params=params(),
        cost_estimate=pl.CostEstimate(
            flops=10 * H * ROWS * SEQ * DH * 4, bytes_accessed=5 << 20, transcendentals=H * ROWS * SEQ
        ),
        name="full_backward",
    )(lengths, ctx, query, kv, kv, out_t, grad_t, lse, *early)


def band_kernel(len_ref, ctx_ref, q_ref, k_ref, v_ref, g_ref, o_ref, dq_ref, dkv_ref):
    first_row = ctx_ref[0, 0] * ROWS
    rows = first_row + lax.broadcasted_iota(jnp.int32, (1, ROWS), 1)
    starts = jnp.maximum(row_starts(len_ref, rows), rows - (BAND - 1))
    bias = mask_of(starts, rows, first_row - BAND)
    keys, values = k_ref[...], v_ref[...]
    key_terms, value_terms = [], []
    for s in range(2):
        query, grad = stacked(q_ref, s, SCALE), stacked(g_ref, s)
        scores = nt(both_lanes(keys, s), query)
        turned = head_transposed(values, s)
        weights, low_weights, outs = [], [], []
        for parity in range(2):
            part = scores[parity * KB : (parity + 1) * KB] + bias
            grown = jnp.exp(part - jnp.max(part, axis=0, keepdims=True))
            grown = grown * (1.0 / jnp.sum(grown, axis=0, keepdims=True))
            weights.append(grown)
            low_weights.append(grown.astype(BF16))
            outs.append(nn(turned, low_weights[parity]))
        store_rows(o_ref, jnp.concatenate(outs, axis=0), s)
        corr = corrections(g_ref, o_ref, s)
        grad_weights = nt(both_lanes(values, s), grad)
        turned = head_transposed(keys, s)
        grad_scores, grad_query = [], []
        for parity in range(2):
            half = slice(parity * KB, (parity + 1) * KB)
            term = (weights[parity] * (grad_weights[half] - corr[parity])).astype(BF16)
            grad_scores.append(term)
            grad_query.append(nn(turned, term))
        store_rows(dq_ref, jnp.concatenate(grad_query, axis=0) * SCALE, s)
        key_terms.append(nn(jnp.concatenate(grad_scores, axis=0), query))
        value_terms.append(nn(jnp.concatenate(low_weights, axis=0), grad))
    dkv_ref[0, :, :128] = head_pair(*key_terms)
    dkv_ref[0, :, 128:] = head_pair(*value_terms)


def banded_layer(lengths, ctx, projected, kv_ext, grad):
    return pl.pallas_call(
        band_kernel,
        grid=(2,),
        in_specs=[
            smem(),
            smem(),
            wide_spec(),
            pl.BlockSpec((KB, 128), lambda g: (0, g)),
            pl.BlockSpec((KB, 128), lambda g: (0, 2 + g)),
            wide_spec(),
        ],
        out_specs=[wide_spec(), wide_spec(), pl.BlockSpec((1, KB, 256), lambda g: (g, 0, 0))],
        out_shape=[
            jax.ShapeDtypeStruct((ROWS, H * DH), BF16),
            jax.ShapeDtypeStruct((ROWS, H * DH), BF16),
            jax.ShapeDtypeStruct((2, KB, 256), F32),
        ],
        compiler_params=params(),
        cost_estimate=pl.CostEstimate(flops=14 * H * ROWS * KB * DH * 4, bytes_accessed=5 << 20, transcendentals=H * ROWS * KB),
        name="banded_layer",
    )(lengths, ctx, projected, kv_ext, kv_ext, grad)


def shifted(value, axis, count, step):
    return lax.ppermute(value, axis, [(i, (i + step) % count) for i in range(count)])


def swapped(value):
    return shifted(value, "c", 2, 1)


def steps_of(count):
    return sorted(range(1, count), key=lambda r: -min(r, count - r))


def sent_chunks(chunk, axis, count):
    me = lax.axis_index(axis)
    sends = [chunk(lax.rem(me + r, count)) for r in steps_of(count)]
    return sends, [shifted(send, axis, count, r) for send, r in zip(sends, steps_of(count))]


def summed(parts):
    total = parts[0].astype(F32)
    for part in parts[1:]:
        total = total + part.astype(F32)
    return total.astype(BF16)


def after(values, event):
    held, _ = lax.optimization_barrier((values, event))
    return held


def by_columns_kernel(rows_ref, early, out_ref):
    for y in range(4):
        out_ref[y] = rows_ref[:, y * 640 : (y + 1) * 640]


def by_columns(rows, early):
    return pl.pallas_call(
        by_columns_kernel,
        in_specs=[vmem(), pl.BlockSpec(memory_space=pl.ANY)],
        out_specs=vmem(),
        out_shape=jax.ShapeDtypeStruct((4, 192, 640), BF16),
        compiler_params=pltpu.CompilerParams(vmem_limit_bytes=VMEM_LIMIT),
        cost_estimate=pl.CostEstimate(flops=0, bytes_accessed=2 << 20, transcendentals=0),
        name="by_columns",
    )(rows, early)


def exchanged(value, axis, dim=0):
    return lax.all_to_all(value, axis, split_axis=dim, concat_axis=dim)


def gathered(value, axis, count):
    return exchanged(jnp.broadcast_to(value[None], (count, *value.shape)), axis)


def pick(array, index):
    return lax.dynamic_index_in_dim(array, index, 0, keepdims=False)


def first_gather(w_out, w_qkv, event, later):
    eighth = pick(w_out.reshape(8, 8, 1440), lax.axis_index(CTX))
    eighth = column_groups(jnp.pad(eighth, ((0, 0), (0, 96))))
    rows = pick(jnp.pad(w_qkv[:, CUT:], ((0, 3), (0, 0))).reshape(2, 24, 1536), lax.axis_index("xh"))
    rows = column_groups(lax.dynamic_slice_in_dim(rows, (lax.axis_index("y") + nothing(event)) * 384, 384, 1))
    both = gathered(jnp.concatenate([eighth, rows], axis=0), "z", 8)
    eighth = lax.dynamic_slice_in_dim(both, nothing(later), 96, 1)
    out_piece = gathered_round_x(from_column_groups(eighth, 8))
    rows = lax.dynamic_slice_in_dim(both, nothing(out_piece) + 96, 72, 1)
    return out_piece, from_column_groups(rows, 24)


def nothing(values):
    first = lax.slice(values, (0,) * values.ndim, (1,) * values.ndim).reshape(())
    return jnp.minimum(jnp.abs(first.astype(jnp.int32)), 0)


def gathered_round_x(piece):
    me = lax.axis_index(X)
    whole = jnp.broadcast_to(piece[:, None, None], (8, 2, 2, 8, 1536))
    for r in steps_of(4):
        source = lax.rem(me - r + 4, 4)
        part = shifted(piece, X, 4, r).reshape(8, 1, 1, 8, 1536)
        whole = lax.dynamic_update_slice(whole, part, (0, lax.rem(source, 2), lax.div(source, 2), 0, 0))
    return whole


def sent_round(value, axis, count):
    return [shifted(value, axis, count, r) for r in steps_of(count)]


def ring_sources(axis, count):
    me = lax.axis_index(axis)
    return [me] + [lax.rem(me - r + count, count) for r in steps_of(count)]


def views(refs):
    return [ref.at[i] for ref in refs for i in range(ref.shape[0])]


def weighted_kernel(count, at_ref, terms_ref, *refs):
    parts, out_ref, turned = views(refs[:count]), refs[-2], refs[-1]
    depth, width = parts[0].shape
    for i in range(8):
        mine = terms_ref[at_ref[0, i // 4], at_ref[0, 2 + i % 4]]
        turned[i, :, :depth] = jnp.transpose(mine.astype(F32)).astype(BF16)
    for tile in range(width // 256):
        at = slice(tile * 256, (tile + 1) * 256)
        total = nn(turned[0, :, :depth], parts[0][:, at])
        for i in range(1, 8):
            total = total + nn(turned[i, :, :depth], parts[i][:, at])
        out_ref[:, at] = total.astype(out_ref.dtype)


def vmem():
    return pl.BlockSpec(memory_space=pltpu.VMEM)


def weighted(at, terms, parts, dtype):
    _, depth, width = parts[0].shape
    return pl.pallas_call(
        functools.partial(weighted_kernel, len(parts)),
        in_specs=[smem()] + [vmem()] * (len(parts) + 1),
        out_specs=vmem(),
        out_shape=jax.ShapeDtypeStruct((ROWS, width), dtype),
        scratch_shapes=[pltpu.VMEM((8, ROWS, 256), BF16)],
        compiler_params=pltpu.CompilerParams(vmem_limit_bytes=VMEM_LIMIT),
        cost_estimate=pl.CostEstimate(
            flops=16 * depth * width * ROWS, bytes_accessed=16 * depth * width, transcendentals=0
        ),
        name="weighted",
    )(at, terms, *parts)


def back_through_kernel(count, at_ref, grad_ref, *refs):
    parts, out_ref = views(refs[:count]), refs[-1]
    for i in range(8):
        out_ref[at_ref[0, i // 4], at_ref[0, 2 + i % 4]] = nt(parts[i][...], grad_ref[...]).astype(out_ref.dtype)


def back_through(at, grad, parts, dtype, early):
    _, depth, width = parts[0].shape
    return pl.pallas_call(
        functools.partial(back_through_kernel, len(parts)),
        in_specs=[smem()] + [vmem()] * (len(parts) + 1) + [pl.BlockSpec(memory_space=pl.ANY)],
        out_specs=vmem(),
        out_shape=jax.ShapeDtypeStruct((2, 4, depth, ROWS), dtype),
        compiler_params=pltpu.CompilerParams(vmem_limit_bytes=VMEM_LIMIT),
        cost_estimate=pl.CostEstimate(
            flops=16 * depth * width * ROWS, bytes_accessed=16 * depth * width, transcendentals=0
        ),
        name="back_through",
    )(at, grad, *parts, early)


def column_groups(rows):
    *lead, r, width = rows.shape
    n = width // 128
    return jnp.swapaxes(rows.reshape(*lead, r, n, 128), -3, -2).reshape(*lead, n * r, 128)


def from_column_groups(groups, r):
    *lead, size, _ = groups.shape
    n = size // r
    return jnp.swapaxes(groups.reshape(*lead, n, r, 128), -3, -2).reshape(*lead, r, n * 128)


def per_device(query_a, key_a, value_a, resid_in, doc_lengths, w_out, w_qkv, grad_out, grad_resid):
    core = lax.axis_index("c")
    ctx = lax.axis_index(CTX).reshape(1, 1)
    lengths = doc_lengths
    w_b0 = lax.all_gather(jnp.pad(w_qkv[:, :CUT], ((0, 3), (0, 0))), FSDP, axis=0, tiled=True)
    own_kv = jnp.concatenate([key_a[0], value_a[0]], axis=1)
    kv = gathered(own_kv, CTX, 8).reshape(SEQ, 512)
    query = query_a[0]
    attended_t, lse = full_forward(lengths, ctx, query, kv)
    out_piece, qkv_piece = first_gather(w_out, w_qkv, kv, lse)
    out_parts = sent_round(out_piece, "y", 4)
    columns = gathered(qkv_piece, "y", 4)
    qkv_piece = jnp.concatenate([pick(columns, nothing(w_b0)), *columns[1:]], axis=2).reshape(192, 1536)
    own_w = lax.all_gather(qkv_piece, X, axis=0, tiled=True).reshape(4, 192, 1536)
    own_o = [part.reshape(1, 256, 1536) for part in [out_piece, *out_parts]]
    other_o = [swapped(part) for part in own_o]
    both_o, both_w = own_o + other_o, [own_w, swapped(own_w)]
    at_y = jnp.stack([core, 1 - core, *ring_sources("y", 4)]).astype(jnp.int32).reshape(1, 6)
    at_x = jnp.stack([core, 1 - core, 0, 1, 2, 3]).astype(jnp.int32).reshape(1, 6)
    attended_t = attended_t.reshape(2, 1024, ROWS)
    own_t, other_t = pick(attended_t, core), pick(attended_t, 1 - core)
    pair_attended = jnp.concatenate([own_t, swapped(other_t)], axis=1)
    by_y = attended_t.reshape(2, 8, 2, 2, 4, 8, ROWS).transpose(0, 4, 1, 2, 3, 5, 6).reshape(2, 4, 256, ROWS)
    product = weighted(at_y, by_y, both_o, F32)[:, :1440]
    resid_mid = (resid_in[0].astype(F32) + product).astype(BF16)
    resid_f = resid_mid.astype(F32)
    inverse_rms = lax.rsqrt(jnp.mean(resid_f * resid_f, axis=-1, keepdims=True) + EPSILON)
    normed = resid_f * inverse_rms
    normed_bf = normed.astype(BF16)
    turned = jnp.pad(normed_bf.T.reshape(32, 45, ROWS), ((0, 0), (0, 3), (0, 0)))
    padded = turned.reshape(1536, ROWS)
    turned = turned.reshape(8, 2, 2, 2, 24, ROWS).transpose(2, 3, 1, 0, 4, 5).reshape(2, 768, ROWS)
    own_n = pick(turned, core)
    sent_normed = pick(turned, 1 - core)
    pair_normed = jnp.concatenate([own_n, swapped(sent_normed)], axis=1)
    padded = after(padded, sent_normed)
    projected = jnp.concatenate(
        [
            tn(padded, w_b0).astype(BF16),
            weighted(at_x, turned.reshape(2, 4, 192, ROWS), both_w, BF16),
        ],
        axis=1,
    )
    own_b = projected[:, H * DH :]
    tail = shifted(own_b, CTX, 8, 1)
    kv_ext = jnp.concatenate([tail, own_b], axis=0)
    banded, grad_qb, kv_grad = banded_layer(lengths, ctx, projected, kv_ext, grad_out[0])
    head = shifted(kv_grad[:, :BAND].astype(BF16), CTX, 8, -1).astype(F32)
    last = lax.axis_index(CTX) == 7
    own_grad = (kv_grad[:, BAND:] + jnp.where(last, 0.0, head)).astype(BF16)
    grad_proj = jnp.concatenate(
        [grad_qb, own_grad[0, :, :128], own_grad[1, :, :128], own_grad[0, :, 128:], own_grad[1, :, 128:]],
        axis=1,
    )
    pair_proj = jnp.concatenate([grad_proj, swapped(grad_proj)], axis=0)
    first = nn(pair_normed, pair_proj).astype(BF16).reshape(4, 192, 2560)
    first_sent = first
    first = lax.psum_scatter(first, X, scatter_dimension=0, tiled=False)
    grad_turned = nt(w_b0, grad_proj[:, :CUT])
    rest = back_through(at_x, grad_proj[:, CUT:], both_w, F32, first_sent)
    rest = rest.reshape(2, 2, 2, 8, 24, ROWS).transpose(3, 2, 0, 1, 4, 5).reshape(32, 48, ROWS)
    grad_turned = (grad_turned.reshape(32, 48, ROWS) + rest)[:, :45].reshape(1440, ROWS)
    grad_normed = grad_turned.T
    middle = jnp.mean(grad_normed * normed, axis=-1, keepdims=True)
    grad_mid = (
        grad_resid[0].astype(F32) + inverse_rms * (grad_normed - normed * middle)
    ).astype(BF16)
    wide_mid = jnp.pad(grad_mid, ((0, 0), (0, 96)))
    pair_mid = jnp.concatenate([wide_mid, swapped(wide_mid)], axis=0)
    sent_out = jnp.stack([nn(pair_attended, pair_mid[:, y * 384 : (y + 1) * 384]).astype(BF16) for y in range(4)])
    me_y = lax.axis_index("y")
    out_sends = [pick(sent_out, lax.rem(me_y + r, 4)) for r in steps_of(4)]
    out_first = [shifted(send, "y", 4, r) for send, r in zip(out_sends, steps_of(4))]
    out_first.append(pick(sent_out, me_y))
    grad_t = back_through(at_y, wide_mid, both_o, BF16, out_sends[-1])
    grad_t = grad_t.reshape(2, 4, 8, 2, 2, 8, ROWS).transpose(0, 2, 3, 4, 1, 5, 6)
    grad_query, kv_terms = full_backward(
        lengths, ctx, query, kv, attended_t.reshape(2, 16, DH, ROWS), grad_t.reshape(2, 16, DH, ROWS), lse, [first_sent, out_sends[-1]]
    )
    kv_terms = exchanged(kv_terms.reshape(2, 8, ROWS, 256), CTX, 1)
    out_first = summed(out_first).reshape(8, 2, 2, 32, 384).transpose(2, 1, 0, 3, 4).reshape(4, 256, 384)
    first = by_columns(first.reshape(192, 2560), out_first)
    second = exchanged(first, "y")
    _, out_second = sent_chunks(lambda i: pick(out_first, i), X, 4)
    out_second.append(pick(out_first, lax.axis_index(X) + nothing(kv_terms)))
    own_terms = jnp.sum(kv_terms.astype(F32), axis=1).astype(BF16)
    grad_key = jnp.concatenate([own_terms[0, :, :128], own_terms[1, :, :128]], axis=1)
    grad_value = jnp.concatenate([own_terms[0, :, 128:], own_terms[1, :, 128:]], axis=1)
    both = jnp.concatenate(
        [
            column_groups(summed(second).reshape(8, 24, 640)),
            column_groups(summed(out_second).reshape(8, 32, 384)),
        ],
        axis=1,
    )
    both = exchanged(both, "z")
    both = jnp.sum(both.astype(F32), axis=0).astype(BF16)
    both = gathered(both, CTX, 8)
    qkv_rows = from_column_groups(both[:, :120], 24).reshape(2, 4, 24, 640)
    grad_w_qkv = qkv_rows.transpose(0, 2, 1, 3).reshape(48, 2560)[:45].astype(F32)
    out_rows = from_column_groups(both[:, 120:], 32).reshape(2, 4, 32, 384)
    grad_w_out = out_rows.transpose(0, 2, 1, 3).reshape(64, 1536)[:, :1440].astype(F32)
    return (
        banded[None],
        grad_mid[None],
        grad_query[None],
        grad_key[None],
        grad_value[None],
        grad_w_out,
        grad_w_qkv,
    )


def solution(mesh):
    torus = jax.sharding.Mesh(mesh.devices.reshape(2, 4, 8, 2, 2), ("xh", "y", "z", "xl", "c"))
    rows = P(FSDP, CTX, None)
    weight = P(FSDP, None)
    return jax.shard_map(
        per_device,
        mesh=torus,
        in_specs=(rows, rows, rows, rows, weight, weight, weight, rows, rows),
        out_specs=(rows, rows, rows, rows, rows, weight, weight),
        check_vma=False,
    )
```

```python
import functools

import jax
import jax.numpy as jnp
import numpy as np
from jax import lax
from jax.experimental import pallas as pl
from jax.experimental.pallas import tpu as pltpu
from jax.sharding import PartitionSpec as P

H = 32
KV = 4
DH = 64
BAND = 128
ROWS = 128
SEQ = 1024
KB = 256
MASKED = -1e30
LOWEST = -1e29
EPSILON = 1e-05
SCALE = DH**-0.5
CTX = ("xh", "y")
FSDP = ("z", "xl", "c")
X = ("xh", "xl")
F32 = jnp.float32
BF16 = jnp.bfloat16
VMEM_LIMIT = 48 * 1024 * 1024


def nt(a, b):
    return lax.dot_general(a, b, (((1,), (1,)), ((), ())), preferred_element_type=F32)


def nn(a, b):
    return lax.dot_general(a, b, (((1,), (0,)), ((), ())), preferred_element_type=F32)


def tn(a, b):
    return lax.dot_general(a, b, (((0,), (0,)), ((), ())), preferred_element_type=F32)


def row_starts(len_ref, rows):
    start, end = jnp.zeros_like(rows), 0
    for d in range(6):
        size = len_ref[0, d]
        end = end + size
        start = start + jnp.where(rows >= end, size, 0)
    return start


def scalar_start(len_ref, row):
    start, end = 0, 0
    for d in range(6):
        size = len_ref[0, d]
        end = end + size
        start = start + jnp.where(row >= end, size, 0)
    return start


def both_lanes(block, s):
    wide = block.astype(F32)
    lane = lax.broadcasted_iota(jnp.int32, wide.shape, 1)
    mine = jnp.where((lane < DH) if s == 0 else (lane >= DH), wide, 0.0)
    other = pltpu.roll(mine, DH, 1)
    pair = (mine, other) if s == 0 else (other, mine)
    return jnp.concatenate(pair, axis=0).astype(BF16)


def stacked(ref, s, scale=None):
    parts = [ref[:, s * 512 + p * 128 : s * 512 + (p + 1) * 128] for p in range(4)]
    whole = jnp.concatenate(parts, axis=0)
    if scale is not None:
        whole = whole * jnp.asarray(scale, whole.dtype)
    return whole


def head_transposed(block, s):
    return jnp.transpose(block.astype(F32))[s * DH : (s + 1) * DH].astype(BF16)


def mask_of(starts, rows, first_key):
    keys = first_key + lax.broadcasted_iota(jnp.int32, (KB, ROWS), 0)
    allowed = (keys >= starts) & (keys <= rows)
    bias = jnp.where(allowed, 0.0, MASKED)
    return jnp.concatenate([bias] * 4, axis=1)


def corrections(grad_ref, out_ref, s):
    even, odd = [], []
    for p in range(4):
        at = slice(s * 512 + p * 128, s * 512 + (p + 1) * 128)
        prod = jnp.transpose(grad_ref[:, at].astype(F32) * out_ref[:, at].astype(F32))
        even.append(jnp.sum(prod[:DH], axis=0, keepdims=True))
        odd.append(jnp.sum(prod[DH:], axis=0, keepdims=True))
    return jnp.concatenate(even, axis=1), jnp.concatenate(odd, axis=1)


def store_rows(ref, transposed, s):
    for p in range(4):
        at = slice(s * 512 + p * 128, s * 512 + (p + 1) * 128)
        ref[:, at] = jnp.transpose(transposed[:, p * 128 : (p + 1) * 128]).astype(ref.dtype)


def head_pair(first, second):
    lane = lax.broadcasted_iota(jnp.int32, (KB, 128), 1)
    low = first[:KB] + pltpu.roll(first[KB:], DH, 1)
    high = pltpu.roll(second[:KB], DH, 1) + second[KB:]
    return jnp.where(lane < DH, low, high)


def full_forward_kernel(
    len_ref, ctx_ref, q_ref, k_ref, v_ref, ot_ref, lse_ref, acc, stat
):
    first_row = ctx_ref[0, 0] * ROWS
    rows = first_row + lax.broadcasted_iota(jnp.int32, (1, ROWS), 1)
    starts = row_starts(len_ref, rows)
    low = scalar_start(len_ref, first_row) // KB
    high = (first_row + ROWS + KB - 1) // KB
    acc[...] = jnp.zeros_like(acc)
    stat[:4] = jnp.full((4, 512), LOWEST, F32)
    stat[4:] = jnp.zeros((4, 512), F32)

    def block(b, carry):
        at = pl.ds(pl.multiple_of(b * KB, KB), KB)
        bias = mask_of(starts, rows, b * KB)
        keys, values = k_ref[at, :], v_ref[at, :]
        for s in range(2):
            scores = nt(both_lanes(keys, s), stacked(q_ref, s, SCALE))
            turned = head_transposed(values, s)
            for parity in range(2):
                n = s * 2 + parity
                part = scores[parity * KB : (parity + 1) * KB] + bias
                old = stat[n : n + 1]
                new = jnp.maximum(old, jnp.max(part, axis=0, keepdims=True))
                weights = jnp.exp(part - new)
                fade = jnp.exp(old - new)
                stat[n : n + 1] = new
                stat[4 + n : 5 + n] = stat[4 + n : 5 + n] * fade + jnp.sum(weights, axis=0, keepdims=True)
                acc[n] = acc[n] * fade + nn(turned, weights.astype(BF16))
        return carry

    lax.fori_loop(low, high, block, 0)
    lse_ref[0] = jnp.concatenate([stat[:4] + jnp.log(stat[4:]), jnp.zeros((4, 512), F32)], axis=0)
    for s in range(2):
        halves = [acc[s * 2 + n] * (1.0 / stat[4 + s * 2 + n : 5 + s * 2 + n]) for n in range(2)]
        for parity in range(2):
            for p in range(4):
                ot_ref[parity, s * 4 + p] = halves[parity][:, p * 128 : (p + 1) * 128].astype(BF16)


def smem():
    return pl.BlockSpec(memory_space=pltpu.SMEM)


def params():
    return pltpu.CompilerParams(
        vmem_limit_bytes=VMEM_LIMIT, dimension_semantics=("arbitrary",)
    )


def wide_spec():
    return pl.BlockSpec((ROWS, 1024), lambda g: (0, g))


def full_forward(lengths, ctx, query, kv):
    return pl.pallas_call(
        full_forward_kernel,
        grid=(2,),
        in_specs=[
            smem(),
            smem(),
            wide_spec(),
            pl.BlockSpec((SEQ, 128), lambda g: (0, g)),
            pl.BlockSpec((SEQ, 128), lambda g: (0, 2 + g)),
        ],
        out_specs=[
            turned_spec(),
            pl.BlockSpec((1, 8, 512), lambda g: (g, 0, 0)),
        ],
        out_shape=[
            jax.ShapeDtypeStruct((2, 16, DH, ROWS), BF16),
            jax.ShapeDtypeStruct((2, 8, 512), F32),
        ],
        scratch_shapes=[pltpu.VMEM((4, DH, 512), F32), pltpu.VMEM((8, 512), F32)],
        compiler_params=params(),
        cost_estimate=pl.CostEstimate(flops=4 * H * ROWS * SEQ * DH * 4, bytes_accessed=3 << 20, transcendentals=H * ROWS * SEQ),
        name="full_forward",
    )(lengths, ctx, query, kv, kv)


def full_backward_kernel(
    len_ref, ctx_ref, q_ref, k_ref, v_ref, o_ref, g_ref, lse_ref, early_a, early_b, dq_ref, dkv_ref, acc, corr, grads
):
    first_row = ctx_ref[0, 0] * ROWS
    rows = first_row + lax.broadcasted_iota(jnp.int32, (1, ROWS), 1)
    starts = row_starts(len_ref, rows)
    low = scalar_start(len_ref, first_row) // KB
    high = (first_row + ROWS + KB - 1) // KB
    acc[...] = jnp.zeros_like(acc)
    dkv_ref[...] = jnp.zeros_like(dkv_ref)
    for s in range(2):
        for p in range(4):
            at = slice(p * 128, (p + 1) * 128)
            halves = [g_ref[parity, s * 4 + p].astype(F32) for parity in range(2)]
            grads[s, at, :] = jnp.transpose(jnp.concatenate(halves, axis=0)).astype(BF16)
            for parity in range(2):
                product = halves[parity] * o_ref[parity, s * 4 + p].astype(F32)
                n = s * 2 + parity
                corr[n : n + 1, at] = jnp.sum(product, axis=0, keepdims=True)

    def block(b, carry):
        at = pl.ds(pl.multiple_of(b * KB, KB), KB)
        bias = mask_of(starts, rows, b * KB)
        keys, values = k_ref[at, :], v_ref[at, :]
        key_terms, value_terms = [], []
        for s in range(2):
            query, grad = stacked(q_ref, s, SCALE), grads[s]
            scores = nt(both_lanes(keys, s), query)
            grad_weights = nt(both_lanes(values, s), grad)
            turned = head_transposed(keys, s)
            low_weights, grad_scores = [], []
            for parity in range(2):
                n = s * 2 + parity
                half = slice(parity * KB, (parity + 1) * KB)
                weights = jnp.exp(scores[half] + bias - lse_ref[0, n : n + 1])
                low_weights.append(weights.astype(BF16))
                term = (weights * (grad_weights[half] - corr[n : n + 1])).astype(BF16)
                grad_scores.append(term)
                acc[n] += nn(turned, term)
            key_terms.append(nn(jnp.concatenate(grad_scores, axis=0), query))
            value_terms.append(nn(jnp.concatenate(low_weights, axis=0), grad))
        dkv_ref[0, at, :128] = head_pair(*key_terms).astype(BF16)
        dkv_ref[0, at, 128:] = head_pair(*value_terms).astype(BF16)
        return carry

    lax.fori_loop(low, high, block, 0)
    for s in range(2):
        store_rows(dq_ref, jnp.concatenate([acc[s * 2], acc[s * 2 + 1]], axis=0) * SCALE, s)


def turned_spec():
    return pl.BlockSpec((2, 8, DH, ROWS), lambda g: (0, g, 0, 0))


def full_backward(lengths, ctx, query, kv, out_t, grad_t, lse, early):
    return pl.pallas_call(
        full_backward_kernel,
        grid=(2,),
        in_specs=[
            smem(),
            smem(),
            wide_spec(),
            pl.BlockSpec((SEQ, 128), lambda g: (0, g)),
            pl.BlockSpec((SEQ, 128), lambda g: (0, 2 + g)),
            turned_spec(),
            turned_spec(),
            pl.BlockSpec((1, 8, 512), lambda g: (g, 0, 0)),
            pl.BlockSpec(memory_space=pl.ANY),
            pl.BlockSpec(memory_space=pl.ANY),
        ],
        out_specs=[wide_spec(), pl.BlockSpec((1, SEQ, 256), lambda g: (g, 0, 0))],
        out_shape=[
            jax.ShapeDtypeStruct((ROWS, H * DH), BF16),
            jax.ShapeDtypeStruct((2, SEQ, 256), BF16),
        ],
        scratch_shapes=[
            pltpu.VMEM((4, DH, 512), F32),
            pltpu.VMEM((8, 512), F32),
            pltpu.VMEM((2, 512, 128), BF16),
        ],
        compiler_params=params(),
        cost_estimate=pl.CostEstimate(
            flops=10 * H * ROWS * SEQ * DH * 4, bytes_accessed=5 << 20, transcendentals=H * ROWS * SEQ
        ),
        name="full_backward",
    )(lengths, ctx, query, kv, kv, out_t, grad_t, lse, *early)


def band_kernel(len_ref, ctx_ref, q_ref, k_ref, v_ref, g_ref, o_ref, dq_ref, dkv_ref):
    first_row = ctx_ref[0, 0] * ROWS
    rows = first_row + lax.broadcasted_iota(jnp.int32, (1, ROWS), 1)
    starts = jnp.maximum(row_starts(len_ref, rows), rows - (BAND - 1))
    bias = mask_of(starts, rows, first_row - BAND)
    keys, values = k_ref[...], v_ref[...]
    key_terms, value_terms = [], []
    for s in range(2):
        query, grad = stacked(q_ref, s, SCALE), stacked(g_ref, s)
        scores = nt(both_lanes(keys, s), query)
        turned = head_transposed(values, s)
        weights, low_weights, outs = [], [], []
        for parity in range(2):
            part = scores[parity * KB : (parity + 1) * KB] + bias
            grown = jnp.exp(part - jnp.max(part, axis=0, keepdims=True))
            grown = grown * (1.0 / jnp.sum(grown, axis=0, keepdims=True))
            weights.append(grown)
            low_weights.append(grown.astype(BF16))
            outs.append(nn(turned, low_weights[parity]))
        store_rows(o_ref, jnp.concatenate(outs, axis=0), s)
        corr = corrections(g_ref, o_ref, s)
        grad_weights = nt(both_lanes(values, s), grad)
        turned = head_transposed(keys, s)
        grad_scores, grad_query = [], []
        for parity in range(2):
            half = slice(parity * KB, (parity + 1) * KB)
            term = (weights[parity] * (grad_weights[half] - corr[parity])).astype(BF16)
            grad_scores.append(term)
            grad_query.append(nn(turned, term))
        store_rows(dq_ref, jnp.concatenate(grad_query, axis=0) * SCALE, s)
        key_terms.append(nn(jnp.concatenate(grad_scores, axis=0), query))
        value_terms.append(nn(jnp.concatenate(low_weights, axis=0), grad))
    dkv_ref[0, :, :128] = head_pair(*key_terms)
    dkv_ref[0, :, 128:] = head_pair(*value_terms)


def banded_layer(lengths, ctx, projected, kv_ext, grad):
    return pl.pallas_call(
        band_kernel,
        grid=(2,),
        in_specs=[
            smem(),
            smem(),
            wide_spec(),
            pl.BlockSpec((KB, 128), lambda g: (0, g)),
            pl.BlockSpec((KB, 128), lambda g: (0, 2 + g)),
            wide_spec(),
        ],
        out_specs=[wide_spec(), wide_spec(), pl.BlockSpec((1, KB, 256), lambda g: (g, 0, 0))],
        out_shape=[
            jax.ShapeDtypeStruct((ROWS, H * DH), BF16),
            jax.ShapeDtypeStruct((ROWS, H * DH), BF16),
            jax.ShapeDtypeStruct((2, KB, 256), F32),
        ],
        compiler_params=params(),
        cost_estimate=pl.CostEstimate(flops=14 * H * ROWS * KB * DH * 4, bytes_accessed=5 << 20, transcendentals=H * ROWS * KB),
        name="banded_layer",
    )(lengths, ctx, projected, kv_ext, kv_ext, grad)


def shifted(value, axis, count, step):
    return lax.ppermute(value, axis, [(i, (i + step) % count) for i in range(count)])


def swapped(value):
    return shifted(value, "c", 2, 1)


def steps_of(count):
    return sorted(range(1, count), key=lambda r: -min(r, count - r))


def sent_chunks(chunk, axis, count):
    me = lax.axis_index(axis)
    sends = [chunk(lax.rem(me + r, count)) for r in steps_of(count)]
    return sends, [shifted(send, axis, count, r) for send, r in zip(sends, steps_of(count))]


def summed(parts):
    total = parts[0].astype(F32)
    for part in parts[1:]:
        total = total + part.astype(F32)
    return total.astype(BF16)


def after(values, event):
    held, _ = lax.optimization_barrier((values, event))
    return held


def by_columns_kernel(rows_ref, early, out_ref):
    for y in range(4):
        out_ref[y] = rows_ref[:, y * 640 : (y + 1) * 640]


def by_columns(rows, early):
    return pl.pallas_call(
        by_columns_kernel,
        in_specs=[vmem(), pl.BlockSpec(memory_space=pl.ANY)],
        out_specs=vmem(),
        out_shape=jax.ShapeDtypeStruct((4, 192, 640), BF16),
        compiler_params=pltpu.CompilerParams(vmem_limit_bytes=VMEM_LIMIT),
        cost_estimate=pl.CostEstimate(flops=0, bytes_accessed=2 << 20, transcendentals=0),
        name="by_columns",
    )(rows, early)


def exchanged(value, axis, dim=0):
    return lax.all_to_all(value, axis, split_axis=dim, concat_axis=dim)


def gathered(value, axis, count):
    return exchanged(jnp.broadcast_to(value[None], (count, *value.shape)), axis)


def pick(array, index):
    return lax.dynamic_index_in_dim(array, index, 0, keepdims=False)


def nothing(values):
    first = lax.slice(values, (0,) * values.ndim, (1,) * values.ndim).reshape(())
    return jnp.minimum(jnp.abs(first.astype(jnp.int32)), 0)


def gathered_round_x(piece):
    me = lax.axis_index(X)
    whole = jnp.broadcast_to(piece[:, None, None], (8, 2, 2, 8, 1536))
    for r in steps_of(4):
        source = lax.rem(me - r + 4, 4)
        part = shifted(piece, X, 4, r).reshape(8, 1, 1, 8, 1536)
        whole = lax.dynamic_update_slice(whole, part, (0, lax.rem(source, 2), lax.div(source, 2), 0, 0))
    return whole


def sent_round(value, axis, count):
    return [shifted(value, axis, count, r) for r in steps_of(count)]


def ring_sources(axis, count):
    me = lax.axis_index(axis)
    return [me] + [lax.rem(me - r + count, count) for r in steps_of(count)]


def views(refs):
    return [ref.at[i] for ref in refs for i in range(ref.shape[0])]


def weighted_kernel(count, at_ref, terms_ref, *refs):
    parts, out_ref, turned = views(refs[:count]), refs[-2], refs[-1]
    depth, width = parts[0].shape
    for i in range(8):
        mine = terms_ref[at_ref[0, i // 4], at_ref[0, 2 + i % 4]]
        turned[i, :, :depth] = jnp.transpose(mine.astype(F32)).astype(BF16)
    for tile in range(width // 256):
        at = slice(tile * 256, (tile + 1) * 256)
        total = nn(turned[0, :, :depth], parts[0][:, at])
        for i in range(1, 8):
            total = total + nn(turned[i, :, :depth], parts[i][:, at])
        out_ref[:, at] = total.astype(out_ref.dtype)


def vmem():
    return pl.BlockSpec(memory_space=pltpu.VMEM)


def weighted(at, terms, parts, dtype):
    _, depth, width = parts[0].shape
    return pl.pallas_call(
        functools.partial(weighted_kernel, len(parts)),
        in_specs=[smem()] + [vmem()] * (len(parts) + 1),
        out_specs=vmem(),
        out_shape=jax.ShapeDtypeStruct((ROWS, width), dtype),
        scratch_shapes=[pltpu.VMEM((8, ROWS, 256), BF16)],
        compiler_params=pltpu.CompilerParams(vmem_limit_bytes=VMEM_LIMIT),
        cost_estimate=pl.CostEstimate(
            flops=16 * depth * width * ROWS, bytes_accessed=16 * depth * width, transcendentals=0
        ),
        name="weighted",
    )(at, terms, *parts)


def back_through_kernel(count, at_ref, grad_ref, *refs):
    parts, out_ref = views(refs[:count]), refs[-1]
    for i in range(8):
        out_ref[at_ref[0, i // 4], at_ref[0, 2 + i % 4]] = nt(parts[i][...], grad_ref[...]).astype(out_ref.dtype)


def back_through(at, grad, parts, dtype, early):
    _, depth, width = parts[0].shape
    return pl.pallas_call(
        functools.partial(back_through_kernel, len(parts)),
        in_specs=[smem()] + [vmem()] * (len(parts) + 1) + [pl.BlockSpec(memory_space=pl.ANY)],
        out_specs=vmem(),
        out_shape=jax.ShapeDtypeStruct((2, 4, depth, ROWS), dtype),
        compiler_params=pltpu.CompilerParams(vmem_limit_bytes=VMEM_LIMIT),
        cost_estimate=pl.CostEstimate(
            flops=16 * depth * width * ROWS, bytes_accessed=16 * depth * width, transcendentals=0
        ),
        name="back_through",
    )(at, grad, *parts, early)


def column_groups(rows):
    *lead, r, width = rows.shape
    n = width // 128
    return jnp.swapaxes(rows.reshape(*lead, r, n, 128), -3, -2).reshape(*lead, n * r, 128)


def from_column_groups(groups, r):
    *lead, size, _ = groups.shape
    n = size // r
    return jnp.swapaxes(groups.reshape(*lead, n, r, 128), -3, -2).reshape(*lead, r, n * 128)


def per_device(query_a, key_a, value_a, resid_in, doc_lengths, w_out, w_qkv, grad_out, grad_resid):
    core = lax.axis_index("c")
    ctx = lax.axis_index(CTX).reshape(1, 1)
    lengths = doc_lengths
    w_b = lax.all_gather(jnp.pad(w_qkv, ((0, 3), (0, 0))), FSDP, axis=0, tiled=True)
    eighth = jnp.pad(pick(w_out.reshape(8, 8, 1440), lax.axis_index(CTX)), ((0, 0), (0, 96)))
    out_piece = gathered_round_x(gathered(eighth, "z", 8))
    out_parts = sent_round(out_piece, "y", 4)
    own_kv = jnp.concatenate([key_a[0], value_a[0]], axis=1)
    own_kv = jnp.where(nothing(out_piece) == 0, own_kv, jnp.zeros_like(own_kv))
    kv = gathered(own_kv, CTX, 8).reshape(SEQ, 512)
    query = query_a[0]
    attended_t, lse = full_forward(lengths, ctx, query, kv)
    own_o = [part.reshape(1, 256, 1536) for part in [out_piece, *out_parts]]
    other_o = [swapped(part) for part in own_o]
    both_o = own_o + other_o
    at_y = jnp.stack([core, 1 - core, *ring_sources("y", 4)]).astype(jnp.int32).reshape(1, 6)
    attended_t = attended_t.reshape(2, 1024, ROWS)
    own_t, other_t = pick(attended_t, core), pick(attended_t, 1 - core)
    pair_attended = jnp.concatenate([own_t, swapped(other_t)], axis=1)
    by_y = attended_t.reshape(2, 8, 2, 2, 4, 8, ROWS).transpose(0, 4, 1, 2, 3, 5, 6).reshape(2, 4, 256, ROWS)
    product = weighted(at_y, by_y, both_o, F32)[:, :1440]
    resid_mid = (resid_in[0].astype(F32) + product).astype(BF16)
    resid_f = resid_mid.astype(F32)
    inverse_rms = lax.rsqrt(jnp.mean(resid_f * resid_f, axis=-1, keepdims=True) + EPSILON)
    normed = resid_f * inverse_rms
    normed_bf = normed.astype(BF16)
    turned = jnp.pad(normed_bf.T.reshape(32, 45, ROWS), ((0, 0), (0, 3), (0, 0)))
    padded = turned.reshape(1536, ROWS)
    turned = turned.reshape(8, 2, 2, 2, 24, ROWS).transpose(2, 3, 1, 0, 4, 5).reshape(2, 768, ROWS)
    own_n = pick(turned, core)
    sent_normed = pick(turned, 1 - core)
    pair_normed = jnp.concatenate([own_n, swapped(sent_normed)], axis=1)
    projected = tn(padded, w_b).astype(BF16)
    own_b = projected[:, H * DH :]
    tail = shifted(own_b, CTX, 8, 1)
    kv_ext = jnp.concatenate([tail, own_b], axis=0)
    banded, grad_qb, kv_grad = banded_layer(lengths, ctx, projected, kv_ext, grad_out[0])
    head = shifted(kv_grad[:, :BAND].astype(BF16), CTX, 8, -1).astype(F32)
    swapped_qb = swapped(grad_qb)
    grad_turned = nt(w_b[:, : H * DH], grad_qb)
    last = lax.axis_index(CTX) + nothing(grad_turned) == 7
    own_grad = (kv_grad[:, BAND:] + jnp.where(last, 0.0, head)).astype(BF16)
    grad_kvb = jnp.concatenate(
        [own_grad[0, :, :128], own_grad[1, :, :128], own_grad[0, :, 128:], own_grad[1, :, 128:]], axis=1
    )
    pair_kvb = jnp.concatenate([grad_kvb, swapped(grad_kvb)], axis=0)
    pair_proj = jnp.concatenate([jnp.concatenate([grad_qb, swapped_qb], axis=0), pair_kvb], axis=1)
    first = nn(pair_normed, pair_proj).astype(BF16).reshape(4, 192, 2560)
    first_sent = first
    first = lax.psum_scatter(first, X, scatter_dimension=0, tiled=False)
    grad_turned = grad_turned + nt(w_b[:, H * DH :], grad_kvb)
    grad_turned = grad_turned.reshape(32, 48, ROWS)[:, :45].reshape(1440, ROWS)
    grad_normed = grad_turned.T
    middle = jnp.mean(grad_normed * normed, axis=-1, keepdims=True)
    grad_mid = (
        grad_resid[0].astype(F32) + inverse_rms * (grad_normed - normed * middle)
    ).astype(BF16)
    wide_mid = jnp.pad(grad_mid, ((0, 0), (0, 96)))
    pair_mid = jnp.concatenate([wide_mid, swapped(wide_mid)], axis=0)
    sent_out = jnp.stack([nn(pair_attended, pair_mid[:, y * 384 : (y + 1) * 384]).astype(BF16) for y in range(4)])
    me_y = lax.axis_index("y")
    out_sends = [pick(sent_out, lax.rem(me_y + r, 4)) for r in steps_of(4)]
    out_first = [shifted(send, "y", 4, r) for send, r in zip(out_sends, steps_of(4))]
    out_first.append(pick(sent_out, me_y))
    grad_t = back_through(at_y, wide_mid, both_o, BF16, out_sends[-1])
    grad_t = grad_t.reshape(2, 4, 8, 2, 2, 8, ROWS).transpose(0, 2, 3, 4, 1, 5, 6)
    grad_query, kv_terms = full_backward(
        lengths, ctx, query, kv, attended_t.reshape(2, 16, DH, ROWS), grad_t.reshape(2, 16, DH, ROWS), lse, [first_sent, out_sends[-1]]
    )
    kv_terms = exchanged(kv_terms.reshape(2, 8, ROWS, 256), CTX, 1)
    out_first = summed(out_first).reshape(8, 2, 2, 32, 384).transpose(2, 1, 0, 3, 4).reshape(4, 256, 384)
    first = by_columns(first.reshape(192, 2560), out_first)
    second = exchanged(first, "y")
    _, out_second = sent_chunks(lambda i: pick(out_first, i), X, 4)
    out_second.append(pick(out_first, lax.axis_index(X) + nothing(kv_terms)))
    own_terms = jnp.sum(kv_terms.astype(F32), axis=1).astype(BF16)
    grad_key = jnp.concatenate([own_terms[0, :, :128], own_terms[1, :, :128]], axis=1)
    grad_value = jnp.concatenate([own_terms[0, :, 128:], own_terms[1, :, 128:]], axis=1)
    both = jnp.concatenate(
        [
            column_groups(summed(second).reshape(8, 24, 640)),
            column_groups(summed(out_second).reshape(8, 32, 384)),
        ],
        axis=1,
    )
    both = exchanged(both, "z")
    both = jnp.sum(both.astype(F32), axis=0).astype(BF16)
    both = gathered(both, CTX, 8)
    qkv_rows = from_column_groups(both[:, :120], 24).reshape(2, 4, 24, 640)
    grad_w_qkv = qkv_rows.transpose(0, 2, 1, 3).reshape(48, 2560)[:45].astype(F32)
    out_rows = from_column_groups(both[:, 120:], 32).reshape(2, 4, 32, 384)
    grad_w_out = out_rows.transpose(0, 2, 1, 3).reshape(64, 1536)[:, :1440].astype(F32)
    return (
        banded[None],
        grad_mid[None],
        grad_query[None],
        grad_key[None],
        grad_value[None],
        grad_w_out,
        grad_w_qkv,
    )


def solution(mesh):
    torus = jax.sharding.Mesh(mesh.devices.reshape(2, 4, 8, 2, 2), ("xh", "y", "z", "xl", "c"))
    rows = P(FSDP, CTX, None)
    weight = P(FSDP, None)
    return jax.shard_map(
        per_device,
        mesh=torus,
        in_specs=(rows, rows, rows, rows, weight, weight, weight, rows, rows),
        out_specs=(rows, rows, rows, rows, rows, weight, weight),
        check_vma=False,
    )
```

```python
import functools

import jax
import jax.numpy as jnp
import numpy as np
from jax import lax
from jax.experimental import pallas as pl
from jax.experimental.pallas import tpu as pltpu
from jax.sharding import PartitionSpec as P

H = 32
KV = 4
DH = 64
BAND = 128
ROWS = 128
SEQ = 1024
KB = 256
MASKED = -1e30
LOWEST = -1e29
EPSILON = 1e-05
SCALE = DH**-0.5
CTX = ("xh", "y")
FSDP = ("z", "xl", "c")
X = ("xh", "xl")
F32 = jnp.float32
BF16 = jnp.bfloat16
VMEM_LIMIT = 48 * 1024 * 1024


def nt(a, b):
    return lax.dot_general(a, b, (((1,), (1,)), ((), ())), preferred_element_type=F32)


def nn(a, b):
    return lax.dot_general(a, b, (((1,), (0,)), ((), ())), preferred_element_type=F32)


def tn(a, b):
    return lax.dot_general(a, b, (((0,), (0,)), ((), ())), preferred_element_type=F32)


def row_starts(len_ref, rows):
    start, end = jnp.zeros_like(rows), 0
    for d in range(6):
        size = len_ref[0, d]
        end = end + size
        start = start + jnp.where(rows >= end, size, 0)
    return start


def scalar_start(len_ref, row):
    start, end = 0, 0
    for d in range(6):
        size = len_ref[0, d]
        end = end + size
        start = start + jnp.where(row >= end, size, 0)
    return start


def both_lanes(block, s):
    wide = block.astype(F32)
    lane = lax.broadcasted_iota(jnp.int32, wide.shape, 1)
    mine = jnp.where((lane < DH) if s == 0 else (lane >= DH), wide, 0.0)
    other = pltpu.roll(mine, DH, 1)
    pair = (mine, other) if s == 0 else (other, mine)
    return jnp.concatenate(pair, axis=0).astype(BF16)


def stacked(ref, s, scale=None):
    parts = [ref[:, s * 512 + p * 128 : s * 512 + (p + 1) * 128] for p in range(4)]
    whole = jnp.concatenate(parts, axis=0)
    if scale is not None:
        whole = whole * jnp.asarray(scale, whole.dtype)
    return whole


def head_transposed(block, s):
    return jnp.transpose(block.astype(F32))[s * DH : (s + 1) * DH].astype(BF16)


def mask_of(starts, rows, first_key):
    keys = first_key + lax.broadcasted_iota(jnp.int32, (KB, ROWS), 0)
    allowed = (keys >= starts) & (keys <= rows)
    bias = jnp.where(allowed, 0.0, MASKED)
    return jnp.concatenate([bias] * 4, axis=1)


def corrections(grad_ref, out_ref, s):
    even, odd = [], []
    for p in range(4):
        at = slice(s * 512 + p * 128, s * 512 + (p + 1) * 128)
        prod = jnp.transpose(grad_ref[:, at].astype(F32) * out_ref[:, at].astype(F32))
        even.append(jnp.sum(prod[:DH], axis=0, keepdims=True))
        odd.append(jnp.sum(prod[DH:], axis=0, keepdims=True))
    return jnp.concatenate(even, axis=1), jnp.concatenate(odd, axis=1)


def store_rows(ref, transposed, s):
    for p in range(4):
        at = slice(s * 512 + p * 128, s * 512 + (p + 1) * 128)
        ref[:, at] = jnp.transpose(transposed[:, p * 128 : (p + 1) * 128]).astype(ref.dtype)


def head_pair(first, second):
    lane = lax.broadcasted_iota(jnp.int32, (KB, 128), 1)
    low = first[:KB] + pltpu.roll(first[KB:], DH, 1)
    high = pltpu.roll(second[:KB], DH, 1) + second[KB:]
    return jnp.where(lane < DH, low, high)


def full_forward_kernel(
    len_ref, ctx_ref, q_ref, k_ref, v_ref, ot_ref, lse_ref, acc, stat
):
    first_row = ctx_ref[0, 0] * ROWS
    rows = first_row + lax.broadcasted_iota(jnp.int32, (1, ROWS), 1)
    starts = row_starts(len_ref, rows)
    low = scalar_start(len_ref, first_row) // KB
    high = (first_row + ROWS + KB - 1) // KB
    acc[...] = jnp.zeros_like(acc)
    stat[:4] = jnp.full((4, 512), LOWEST, F32)
    stat[4:] = jnp.zeros((4, 512), F32)

    def block(b, carry):
        at = pl.ds(pl.multiple_of(b * KB, KB), KB)
        bias = mask_of(starts, rows, b * KB)
        keys, values = k_ref[at, :], v_ref[at, :]
        for s in range(2):
            scores = nt(both_lanes(keys, s), stacked(q_ref, s, SCALE))
            turned = head_transposed(values, s)
            for parity in range(2):
                n = s * 2 + parity
                part = scores[parity * KB : (parity + 1) * KB] + bias
                old = stat[n : n + 1]
                new = jnp.maximum(old, jnp.max(part, axis=0, keepdims=True))
                weights = jnp.exp(part - new)
                fade = jnp.exp(old - new)
                stat[n : n + 1] = new
                stat[4 + n : 5 + n] = stat[4 + n : 5 + n] * fade + jnp.sum(weights, axis=0, keepdims=True)
                acc[n] = acc[n] * fade + nn(turned, weights.astype(BF16))
        return carry

    lax.fori_loop(low, high, block, 0)
    lse_ref[0] = jnp.concatenate([stat[:4] + jnp.log(stat[4:]), jnp.zeros((4, 512), F32)], axis=0)
    for s in range(2):
        halves = [acc[s * 2 + n] * (1.0 / stat[4 + s * 2 + n : 5 + s * 2 + n]) for n in range(2)]
        for parity in range(2):
            for p in range(4):
                ot_ref[parity, s * 4 + p] = halves[parity][:, p * 128 : (p + 1) * 128].astype(BF16)


def smem():
    return pl.BlockSpec(memory_space=pltpu.SMEM)


def params():
    return pltpu.CompilerParams(
        vmem_limit_bytes=VMEM_LIMIT, dimension_semantics=("arbitrary",)
    )


def wide_spec():
    return pl.BlockSpec((ROWS, 1024), lambda g: (0, g))


def full_forward(lengths, ctx, query, kv):
    return pl.pallas_call(
        full_forward_kernel,
        grid=(2,),
        in_specs=[
            smem(),
            smem(),
            wide_spec(),
            pl.BlockSpec((SEQ, 128), lambda g: (0, g)),
            pl.BlockSpec((SEQ, 128), lambda g: (0, 2 + g)),
        ],
        out_specs=[
            turned_spec(),
            pl.BlockSpec((1, 8, 512), lambda g: (g, 0, 0)),
        ],
        out_shape=[
            jax.ShapeDtypeStruct((2, 16, DH, ROWS), BF16),
            jax.ShapeDtypeStruct((2, 8, 512), F32),
        ],
        scratch_shapes=[pltpu.VMEM((4, DH, 512), F32), pltpu.VMEM((8, 512), F32)],
        compiler_params=params(),
        cost_estimate=pl.CostEstimate(flops=1 << 16, bytes_accessed=1 << 16, transcendentals=0),
        name="full_forward",
    )(lengths, ctx, query, kv, kv)


def full_backward_kernel(
    len_ref, ctx_ref, q_ref, k_ref, v_ref, o_ref, g_ref, lse_ref, early_a, early_b, dq_ref, dkv_ref, acc, corr, grads
):
    first_row = ctx_ref[0, 0] * ROWS
    rows = first_row + lax.broadcasted_iota(jnp.int32, (1, ROWS), 1)
    starts = row_starts(len_ref, rows)
    low = scalar_start(len_ref, first_row) // KB
    high = (first_row + ROWS + KB - 1) // KB
    acc[...] = jnp.zeros_like(acc)
    dkv_ref[...] = jnp.zeros_like(dkv_ref)
    for s in range(2):
        for p in range(4):
            at = slice(p * 128, (p + 1) * 128)
            halves = [g_ref[parity, s * 4 + p].astype(F32) for parity in range(2)]
            grads[s, at, :] = jnp.transpose(jnp.concatenate(halves, axis=0)).astype(BF16)
            for parity in range(2):
                product = halves[parity] * o_ref[parity, s * 4 + p].astype(F32)
                n = s * 2 + parity
                corr[n : n + 1, at] = jnp.sum(product, axis=0, keepdims=True)

    def block(b, carry):
        at = pl.ds(pl.multiple_of(b * KB, KB), KB)
        bias = mask_of(starts, rows, b * KB)
        keys, values = k_ref[at, :], v_ref[at, :]
        key_terms, value_terms = [], []
        for s in range(2):
            query, grad = stacked(q_ref, s, SCALE), grads[s]
            scores = nt(both_lanes(keys, s), query)
            grad_weights = nt(both_lanes(values, s), grad)
            turned = head_transposed(keys, s)
            low_weights, grad_scores = [], []
            for parity in range(2):
                n = s * 2 + parity
                half = slice(parity * KB, (parity + 1) * KB)
                weights = jnp.exp(scores[half] + bias - lse_ref[0, n : n + 1])
                low_weights.append(weights.astype(BF16))
                term = (weights * (grad_weights[half] - corr[n : n + 1])).astype(BF16)
                grad_scores.append(term)
                acc[n] += nn(turned, term)
            key_terms.append(nn(jnp.concatenate(grad_scores, axis=0), query))
            value_terms.append(nn(jnp.concatenate(low_weights, axis=0), grad))
        dkv_ref[0, at, :128] = head_pair(*key_terms).astype(BF16)
        dkv_ref[0, at, 128:] = head_pair(*value_terms).astype(BF16)
        return carry

    lax.fori_loop(low, high, block, 0)
    for s in range(2):
        store_rows(dq_ref, jnp.concatenate([acc[s * 2], acc[s * 2 + 1]], axis=0) * SCALE, s)


def turned_spec():
    return pl.BlockSpec((2, 8, DH, ROWS), lambda g: (0, g, 0, 0))


def full_backward(lengths, ctx, query, kv, out_t, grad_t, lse, early):
    return pl.pallas_call(
        full_backward_kernel,
        grid=(2,),
        in_specs=[
            smem(),
            smem(),
            wide_spec(),
            pl.BlockSpec((SEQ, 128), lambda g: (0, g)),
            pl.BlockSpec((SEQ, 128), lambda g: (0, 2 + g)),
            turned_spec(),
            turned_spec(),
            pl.BlockSpec((1, 8, 512), lambda g: (g, 0, 0)),
            pl.BlockSpec(memory_space=pl.ANY),
            pl.BlockSpec(memory_space=pl.ANY),
        ],
        out_specs=[wide_spec(), pl.BlockSpec((1, SEQ, 256), lambda g: (g, 0, 0))],
        out_shape=[
            jax.ShapeDtypeStruct((ROWS, H * DH), BF16),
            jax.ShapeDtypeStruct((2, SEQ, 256), BF16),
        ],
        scratch_shapes=[
            pltpu.VMEM((4, DH, 512), F32),
            pltpu.VMEM((8, 512), F32),
            pltpu.VMEM((2, 512, 128), BF16),
        ],
        compiler_params=params(),
        cost_estimate=pl.CostEstimate(
            flops=1 << 16, bytes_accessed=1 << 16, transcendentals=0
        ),
        name="full_backward",
    )(lengths, ctx, query, kv, kv, out_t, grad_t, lse, *early)


def band_kernel(len_ref, ctx_ref, q_ref, k_ref, v_ref, g_ref, o_ref, dq_ref, dkv_ref):
    first_row = ctx_ref[0, 0] * ROWS
    rows = first_row + lax.broadcasted_iota(jnp.int32, (1, ROWS), 1)
    starts = jnp.maximum(row_starts(len_ref, rows), rows - (BAND - 1))
    bias = mask_of(starts, rows, first_row - BAND)
    keys, values = k_ref[...], v_ref[...]
    key_terms, value_terms = [], []
    for s in range(2):
        query, grad = stacked(q_ref, s, SCALE), stacked(g_ref, s)
        scores = nt(both_lanes(keys, s), query)
        turned = head_transposed(values, s)
        weights, low_weights, outs = [], [], []
        for parity in range(2):
            part = scores[parity * KB : (parity + 1) * KB] + bias
            grown = jnp.exp(part - jnp.max(part, axis=0, keepdims=True))
            grown = grown * (1.0 / jnp.sum(grown, axis=0, keepdims=True))
            weights.append(grown)
            low_weights.append(grown.astype(BF16))
            outs.append(nn(turned, low_weights[parity]))
        store_rows(o_ref, jnp.concatenate(outs, axis=0), s)
        corr = corrections(g_ref, o_ref, s)
        grad_weights = nt(both_lanes(values, s), grad)
        turned = head_transposed(keys, s)
        grad_scores, grad_query = [], []
        for parity in range(2):
            half = slice(parity * KB, (parity + 1) * KB)
            term = (weights[parity] * (grad_weights[half] - corr[parity])).astype(BF16)
            grad_scores.append(term)
            grad_query.append(nn(turned, term))
        store_rows(dq_ref, jnp.concatenate(grad_query, axis=0) * SCALE, s)
        key_terms.append(nn(jnp.concatenate(grad_scores, axis=0), query))
        value_terms.append(nn(jnp.concatenate(low_weights, axis=0), grad))
    dkv_ref[0, :, :128] = head_pair(*key_terms)
    dkv_ref[0, :, 128:] = head_pair(*value_terms)


def banded_layer(lengths, ctx, projected, kv_ext, grad):
    return pl.pallas_call(
        band_kernel,
        grid=(2,),
        in_specs=[
            smem(),
            smem(),
            wide_spec(),
            pl.BlockSpec((KB, 128), lambda g: (0, g)),
            pl.BlockSpec((KB, 128), lambda g: (0, 2 + g)),
            wide_spec(),
        ],
        out_specs=[wide_spec(), wide_spec(), pl.BlockSpec((1, KB, 256), lambda g: (g, 0, 0))],
        out_shape=[
            jax.ShapeDtypeStruct((ROWS, H * DH), BF16),
            jax.ShapeDtypeStruct((ROWS, H * DH), BF16),
            jax.ShapeDtypeStruct((2, KB, 256), F32),
        ],
        compiler_params=params(),
        cost_estimate=pl.CostEstimate(flops=14 * H * ROWS * KB * DH * 4, bytes_accessed=5 << 20, transcendentals=H * ROWS * KB),
        name="banded_layer",
    )(lengths, ctx, projected, kv_ext, kv_ext, grad)


def shifted(value, axis, count, step):
    return lax.ppermute(value, axis, [(i, (i + step) % count) for i in range(count)])


def swapped(value):
    return shifted(value, "c", 2, 1)


def steps_of(count):
    return sorted(range(1, count), key=lambda r: -min(r, count - r))


def sent_chunks(chunk, axis, count):
    me = lax.axis_index(axis)
    sends = [chunk(lax.rem(me + r, count)) for r in steps_of(count)]
    return sends, [shifted(send, axis, count, r) for send, r in zip(sends, steps_of(count))]


def summed(parts):
    total = parts[0].astype(F32)
    for part in parts[1:]:
        total = total + part.astype(F32)
    return total.astype(BF16)


def after(values, event):
    held, _ = lax.optimization_barrier((values, event))
    return held


def by_columns_kernel(rows_ref, early, out_ref):
    for y in range(4):
        out_ref[y] = rows_ref[:, y * 640 : (y + 1) * 640]


def by_columns(rows, early):
    return pl.pallas_call(
        by_columns_kernel,
        in_specs=[vmem(), pl.BlockSpec(memory_space=pl.ANY)],
        out_specs=vmem(),
        out_shape=jax.ShapeDtypeStruct((4, 192, 640), BF16),
        compiler_params=pltpu.CompilerParams(vmem_limit_bytes=VMEM_LIMIT),
        cost_estimate=pl.CostEstimate(flops=0, bytes_accessed=2 << 20, transcendentals=0),
        name="by_columns",
    )(rows, early)


def exchanged(value, axis, dim=0):
    return lax.all_to_all(value, axis, split_axis=dim, concat_axis=dim)


def gathered(value, axis, count):
    return exchanged(jnp.broadcast_to(value[None], (count, *value.shape)), axis)


def pick(array, index):
    return lax.dynamic_index_in_dim(array, index, 0, keepdims=False)


def nothing(values):
    first = lax.slice(values, (0,) * values.ndim, (1,) * values.ndim).reshape(())
    return jnp.minimum(jnp.abs(jnp.clip(first.astype(F32), -1.0, 1.0).astype(jnp.int32)), 0)


def gathered_round_x(piece):
    me = lax.axis_index(X)
    whole = jnp.broadcast_to(piece[:, None, None], (8, 2, 2, 8, 1536))
    for r in steps_of(4):
        source = lax.rem(me - r + 4, 4)
        part = shifted(piece, X, 4, r).reshape(8, 1, 1, 8, 1536)
        whole = lax.dynamic_update_slice(whole, part, (0, lax.rem(source, 2), lax.div(source, 2), 0, 0))
    return whole


def sent_round(value, axis, count):
    return [shifted(value, axis, count, r) for r in steps_of(count)]


def ring_sources(axis, count):
    me = lax.axis_index(axis)
    return [me] + [lax.rem(me - r + count, count) for r in steps_of(count)]


def views(refs):
    return [ref.at[i] for ref in refs for i in range(ref.shape[0])]


def weighted_kernel(count, at_ref, terms_ref, *refs):
    parts, out_ref, turned = views(refs[:count]), refs[-2], refs[-1]
    depth, width = parts[0].shape
    for i in range(8):
        mine = terms_ref[at_ref[0, i // 4], at_ref[0, 2 + i % 4]]
        turned[i, :, :depth] = jnp.transpose(mine.astype(F32)).astype(BF16)
    for tile in range(width // 256):
        at = slice(tile * 256, (tile + 1) * 256)
        total = nn(turned[0, :, :depth], parts[0][:, at])
        for i in range(1, 8):
            total = total + nn(turned[i, :, :depth], parts[i][:, at])
        out_ref[:, at] = total.astype(out_ref.dtype)


def vmem():
    return pl.BlockSpec(memory_space=pltpu.VMEM)


def weighted(at, terms, parts, dtype):
    _, depth, width = parts[0].shape
    return pl.pallas_call(
        functools.partial(weighted_kernel, len(parts)),
        in_specs=[smem()] + [vmem()] * (len(parts) + 1),
        out_specs=vmem(),
        out_shape=jax.ShapeDtypeStruct((ROWS, width), dtype),
        scratch_shapes=[pltpu.VMEM((8, ROWS, 256), BF16)],
        compiler_params=pltpu.CompilerParams(vmem_limit_bytes=VMEM_LIMIT),
        cost_estimate=pl.CostEstimate(
            flops=16 * depth * width * ROWS, bytes_accessed=16 * depth * width, transcendentals=0
        ),
        name="weighted",
    )(at, terms, *parts)


def back_through_kernel(count, at_ref, grad_ref, *refs):
    parts, out_ref = views(refs[:count]), refs[-1]
    for i in range(8):
        out_ref[at_ref[0, i // 4], at_ref[0, 2 + i % 4]] = nt(parts[i][...], grad_ref[...]).astype(out_ref.dtype)


def back_through(at, grad, parts, dtype, early):
    _, depth, width = parts[0].shape
    return pl.pallas_call(
        functools.partial(back_through_kernel, len(parts)),
        in_specs=[smem()] + [vmem()] * (len(parts) + 1) + [pl.BlockSpec(memory_space=pl.ANY)],
        out_specs=vmem(),
        out_shape=jax.ShapeDtypeStruct((2, 4, depth, ROWS), dtype),
        compiler_params=pltpu.CompilerParams(vmem_limit_bytes=VMEM_LIMIT),
        cost_estimate=pl.CostEstimate(
            flops=1 << 16, bytes_accessed=1 << 16, transcendentals=0
        ),
        name="back_through",
    )(at, grad, *parts, early)


def normalised_kernel(product_ref, resid_ref, normed_ref, rms_ref, turned_ref, scratch):
    resid = (resid_ref[...].astype(F32) + product_ref[:, :1440]).astype(BF16).astype(F32)
    rms = lax.rsqrt(jnp.sum(resid * resid, axis=1, keepdims=True) * (1.0 / 1440) + EPSILON)
    normed = resid * rms
    normed_ref[...] = normed
    rms_ref[...] = rms
    scratch[...] = jnp.transpose(jnp.concatenate([normed, jnp.zeros((ROWS, 96), F32)], axis=1))
    row = lax.broadcasted_iota(jnp.int32, (48, ROWS), 0)
    for f in range(32):
        rows = scratch[f * 45 : f * 45 + 48, :]
        turned_ref[f * 48 : (f + 1) * 48, :] = jnp.where(row < 45, rows, 0.0).astype(BF16)


def normalised(product, resid):
    return pl.pallas_call(
        normalised_kernel,
        in_specs=[vmem()] * 2,
        out_specs=[vmem()] * 3,
        out_shape=[
            jax.ShapeDtypeStruct((ROWS, 1440), F32),
            jax.ShapeDtypeStruct((ROWS, 1), F32),
            jax.ShapeDtypeStruct((1536, ROWS), BF16),
        ],
        scratch_shapes=[pltpu.VMEM((1536, ROWS), F32)],
        compiler_params=pltpu.CompilerParams(vmem_limit_bytes=VMEM_LIMIT),
        cost_estimate=pl.CostEstimate(flops=1 << 20, bytes_accessed=3 << 20, transcendentals=0),
        name="normalised",
    )(product, resid)


def through_norm_kernel(turned_ref, normed_ref, rms_ref, resid_ref, grad_ref, wide_ref, scratch):
    for f in range(32):
        scratch[f * 45 : f * 45 + 48, :] = turned_ref[f * 48 : (f + 1) * 48, :]
    scratch[1440:1536, :] = jnp.zeros((96, ROWS), F32)
    grad = jnp.transpose(scratch[...])[:, :1440]
    normed = normed_ref[...]
    middle = jnp.sum(grad * normed, axis=1, keepdims=True) * (1.0 / 1440)
    total = (resid_ref[...].astype(F32) + rms_ref[...] * (grad - normed * middle)).astype(BF16)
    grad_ref[...] = total
    wide_ref[...] = jnp.concatenate([total, jnp.zeros((ROWS, 96), BF16)], axis=1)


def through_norm(turned, normed, inverse_rms, grad_resid):
    return pl.pallas_call(
        through_norm_kernel,
        in_specs=[vmem()] * 4,
        out_specs=[vmem()] * 2,
        out_shape=[
            jax.ShapeDtypeStruct((ROWS, 1440), BF16),
            jax.ShapeDtypeStruct((ROWS, 1536), BF16),
        ],
        scratch_shapes=[pltpu.VMEM((1536, ROWS), F32)],
        compiler_params=pltpu.CompilerParams(vmem_limit_bytes=VMEM_LIMIT),
        cost_estimate=pl.CostEstimate(flops=1 << 20, bytes_accessed=3 << 20, transcendentals=0),
        name="through_norm",
    )(turned, normed, inverse_rms, grad_resid)


def column_groups(rows):
    *lead, r, width = rows.shape
    n = width // 128
    return jnp.swapaxes(rows.reshape(*lead, r, n, 128), -3, -2).reshape(*lead, n * r, 128)


def from_column_groups(groups, r):
    *lead, size, _ = groups.shape
    n = size // r
    return jnp.swapaxes(groups.reshape(*lead, n, r, 128), -3, -2).reshape(*lead, r, n * 128)


def per_device(query_a, key_a, value_a, resid_in, doc_lengths, w_out, w_qkv, grad_out, grad_resid):
    core = lax.axis_index("c")
    ctx = lax.axis_index(CTX).reshape(1, 1)
    lengths = doc_lengths
    w_b = lax.all_gather(jnp.pad(w_qkv, ((0, 3), (0, 0))), FSDP, axis=0, tiled=True)
    eighth = jnp.pad(pick(w_out.reshape(8, 8, 1440), lax.axis_index(CTX)), ((0, 0), (0, 96)))
    out_piece = gathered_round_x(gathered(eighth, "z", 8))
    out_parts = sent_round(out_piece, "y", 4)
    own_kv = jnp.concatenate([key_a[0], value_a[0]], axis=1)
    own_kv = jnp.where(nothing(out_piece) == 0, own_kv, jnp.zeros_like(own_kv))
    kv = gathered(own_kv, CTX, 8).reshape(SEQ, 512)
    query = query_a[0]
    attended_t, lse = full_forward(lengths, ctx, query, kv)
    own_o = [part.reshape(1, 256, 1536) for part in [out_piece, *out_parts]]
    other_o = [swapped(part) for part in own_o]
    both_o = own_o + other_o
    at_y = jnp.stack([core, 1 - core, *ring_sources("y", 4)]).astype(jnp.int32).reshape(1, 6)
    attended_t = attended_t.reshape(2, 1024, ROWS)
    own_t, other_t = pick(attended_t, core), pick(attended_t, 1 - core)
    pair_attended = jnp.concatenate([own_t, swapped(other_t)], axis=1)
    by_y = attended_t.reshape(2, 8, 2, 2, 4, 8, ROWS).transpose(0, 4, 1, 2, 3, 5, 6).reshape(2, 4, 256, ROWS)
    product = weighted(at_y, by_y, both_o, F32)
    normed, inverse_rms, padded = normalised(product, resid_in[0])
    turned = padded
    turned = turned.reshape(8, 2, 2, 2, 24, ROWS).transpose(2, 3, 1, 0, 4, 5).reshape(2, 768, ROWS)
    own_n = pick(turned, core)
    sent_normed = pick(turned, 1 - core)
    pair_normed = jnp.concatenate([own_n, swapped(sent_normed)], axis=1)
    projected = tn(padded, w_b).astype(BF16)
    own_b = projected[:, H * DH :]
    tail = shifted(own_b, CTX, 8, 1)
    kv_ext = jnp.concatenate([tail, own_b], axis=0)
    banded, grad_qb, kv_grad = banded_layer(lengths, ctx, projected, kv_ext, grad_out[0])
    head = shifted(kv_grad[:, :BAND].astype(BF16), CTX, 8, -1).astype(F32)
    swapped_qb = swapped(grad_qb)
    grad_turned = nt(w_b[:, : H * DH], grad_qb)
    last = lax.axis_index(CTX) + nothing(grad_turned) == 7
    own_grad = (kv_grad[:, BAND:] + jnp.where(last, 0.0, head)).astype(BF16)
    grad_kvb = jnp.concatenate(
        [own_grad[0, :, :128], own_grad[1, :, :128], own_grad[0, :, 128:], own_grad[1, :, 128:]], axis=1
    )
    pair_kvb = jnp.concatenate([grad_kvb, swapped(grad_kvb)], axis=0)
    grad_turned = grad_turned + nt(w_b[:, H * DH :], grad_kvb)
    grad_mid, wide_mid = through_norm(grad_turned, normed, inverse_rms, grad_resid[0])
    pair_mid = jnp.concatenate([wide_mid, swapped(wide_mid)], axis=0)
    sent_out = jnp.stack([nn(pair_attended, pair_mid[:, y * 384 : (y + 1) * 384]).astype(BF16) for y in range(4)])
    me_y = lax.axis_index("y")
    out_sends = [pick(sent_out, lax.rem(me_y + r, 4)) for r in steps_of(4)]
    out_first = [shifted(send, "y", 4, r) for send, r in zip(out_sends, steps_of(4))]
    out_first.append(pick(sent_out, me_y))
    pair_proj = jnp.concatenate([jnp.concatenate([grad_qb, swapped_qb], axis=0), pair_kvb], axis=1)
    pair_proj = jnp.where(nothing(sent_out) == 0, pair_proj, jnp.zeros_like(pair_proj))
    first = nn(pair_normed, pair_proj).astype(BF16).reshape(4, 192, 2560)
    first_sent = first
    first = lax.psum_scatter(first, X, scatter_dimension=0, tiled=False)
    grad_t = back_through(at_y, wide_mid, both_o, BF16, out_sends[-1])
    grad_t = grad_t.reshape(2, 4, 8, 2, 2, 8, ROWS).transpose(0, 2, 3, 4, 1, 5, 6)
    grad_query, kv_terms = full_backward(
        lengths, ctx, query, kv, attended_t.reshape(2, 16, DH, ROWS), grad_t.reshape(2, 16, DH, ROWS), lse, [first_sent, out_sends[-1]]
    )
    kv_terms = exchanged(kv_terms.reshape(2, 8, ROWS, 256), CTX, 1)
    out_first = summed(out_first).reshape(8, 2, 2, 32, 384).transpose(2, 1, 0, 3, 4).reshape(4, 256, 384)
    first = by_columns(first.reshape(192, 2560), out_first)
    second = exchanged(first, "y")
    _, out_second = sent_chunks(lambda i: pick(out_first, i), X, 4)
    out_second.append(pick(out_first, lax.axis_index(X) + nothing(kv_terms)))
    own_terms = jnp.sum(kv_terms.astype(F32), axis=1).astype(BF16)
    grad_key = jnp.concatenate([own_terms[0, :, :128], own_terms[1, :, :128]], axis=1)
    grad_value = jnp.concatenate([own_terms[0, :, 128:], own_terms[1, :, 128:]], axis=1)
    both = jnp.concatenate(
        [
            column_groups(summed(second).reshape(8, 24, 640)),
            column_groups(summed(out_second).reshape(8, 32, 384)),
        ],
        axis=1,
    )
    both = exchanged(both, "z")
    both = jnp.sum(both.astype(F32), axis=0).astype(BF16)
    both = gathered(both, CTX, 8)
    qkv_rows = from_column_groups(both[:, :120], 24).reshape(2, 4, 24, 640)
    grad_w_qkv = qkv_rows.transpose(0, 2, 1, 3).reshape(48, 2560)[:45].astype(F32)
    out_rows = from_column_groups(both[:, 120:], 32).reshape(2, 4, 32, 384)
    grad_w_out = out_rows.transpose(0, 2, 1, 3).reshape(64, 1536)[:, :1440].astype(F32)
    return (
        banded[None],
        grad_mid[None],
        grad_query[None],
        grad_key[None],
        grad_value[None],
        grad_w_out,
        grad_w_qkv,
    )


def solution(mesh):
    torus = jax.sharding.Mesh(mesh.devices.reshape(2, 4, 8, 2, 2), ("xh", "y", "z", "xl", "c"))
    rows = P(FSDP, CTX, None)
    weight = P(FSDP, None)
    return jax.shard_map(
        per_device,
        mesh=torus,
        in_specs=(rows, rows, rows, rows, weight, weight, weight, rows, rows),
        out_specs=(rows, rows, rows, rows, rows, weight, weight),
        check_vma=False,
    )
```

```python
import functools

import jax
import jax.numpy as jnp
import numpy as np
from jax import lax
from jax.experimental import pallas as pl
from jax.experimental.pallas import tpu as pltpu
from jax.sharding import PartitionSpec as P

H = 32
KV = 4
DH = 64
BAND = 128
ROWS = 128
SEQ = 1024
KB = 256
MASKED = -1e30
LOWEST = -1e29
EPSILON = 1e-05
SCALE = DH**-0.5
CTX = ("xh", "y")
FSDP = ("z", "xl", "c")
X = ("xh", "xl")
F32 = jnp.float32
BF16 = jnp.bfloat16
VMEM_LIMIT = 48 * 1024 * 1024


def nt(a, b):
    return lax.dot_general(a, b, (((1,), (1,)), ((), ())), preferred_element_type=F32)


def nn(a, b):
    return lax.dot_general(a, b, (((1,), (0,)), ((), ())), preferred_element_type=F32)


def tn(a, b):
    return lax.dot_general(a, b, (((0,), (0,)), ((), ())), preferred_element_type=F32)


def row_starts(len_ref, rows):
    start, end = jnp.zeros_like(rows), 0
    for d in range(6):
        size = len_ref[0, d]
        end = end + size
        start = start + jnp.where(rows >= end, size, 0)
    return start


def scalar_start(len_ref, row):
    start, end = 0, 0
    for d in range(6):
        size = len_ref[0, d]
        end = end + size
        start = start + jnp.where(row >= end, size, 0)
    return start


def both_lanes(block, s):
    wide = block.astype(F32)
    lane = lax.broadcasted_iota(jnp.int32, wide.shape, 1)
    mine = jnp.where((lane < DH) if s == 0 else (lane >= DH), wide, 0.0)
    other = pltpu.roll(mine, DH, 1)
    pair = (mine, other) if s == 0 else (other, mine)
    return jnp.concatenate(pair, axis=0).astype(BF16)


def stacked(ref, s, scale=None):
    parts = [ref[:, s * 512 + p * 128 : s * 512 + (p + 1) * 128] for p in range(4)]
    whole = jnp.concatenate(parts, axis=0)
    if scale is not None:
        whole = whole * jnp.asarray(scale, whole.dtype)
    return whole


def head_transposed(block, s):
    return jnp.transpose(block.astype(F32))[s * DH : (s + 1) * DH].astype(BF16)


def mask_of(starts, rows, first_key):
    keys = first_key + lax.broadcasted_iota(jnp.int32, (KB, ROWS), 0)
    allowed = (keys >= starts) & (keys <= rows)
    bias = jnp.where(allowed, 0.0, MASKED)
    return jnp.concatenate([bias] * 4, axis=1)


def corrections(grad_ref, out_ref, s):
    even, odd = [], []
    for p in range(4):
        at = slice(s * 512 + p * 128, s * 512 + (p + 1) * 128)
        prod = jnp.transpose(grad_ref[:, at].astype(F32) * out_ref[:, at].astype(F32))
        even.append(jnp.sum(prod[:DH], axis=0, keepdims=True))
        odd.append(jnp.sum(prod[DH:], axis=0, keepdims=True))
    return jnp.concatenate(even, axis=1), jnp.concatenate(odd, axis=1)


def store_rows(ref, transposed, s):
    for p in range(4):
        at = slice(s * 512 + p * 128, s * 512 + (p + 1) * 128)
        ref[:, at] = jnp.transpose(transposed[:, p * 128 : (p + 1) * 128]).astype(ref.dtype)


def head_pair(first, second):
    lane = lax.broadcasted_iota(jnp.int32, (KB, 128), 1)
    low = first[:KB] + pltpu.roll(first[KB:], DH, 1)
    high = pltpu.roll(second[:KB], DH, 1) + second[KB:]
    return jnp.where(lane < DH, low, high)


def full_forward_kernel(
    len_ref, ctx_ref, q_ref, k_ref, v_ref, ot_ref, lse_ref, acc, stat
):
    first_row = ctx_ref[0, 0] * ROWS
    rows = first_row + lax.broadcasted_iota(jnp.int32, (1, ROWS), 1)
    starts = row_starts(len_ref, rows)
    low = scalar_start(len_ref, first_row) // KB
    high = (first_row + ROWS + KB - 1) // KB
    acc[...] = jnp.zeros_like(acc)
    stat[:4] = jnp.full((4, 512), LOWEST, F32)
    stat[4:] = jnp.zeros((4, 512), F32)

    def block(b, carry):
        at = pl.ds(pl.multiple_of(b * KB, KB), KB)
        bias = mask_of(starts, rows, b * KB)
        keys, values = k_ref[at, :], v_ref[at, :]
        for s in range(2):
            scores = nt(both_lanes(keys, s), stacked(q_ref, s, SCALE))
            turned = head_transposed(values, s)
            for parity in range(2):
                n = s * 2 + parity
                part = scores[parity * KB : (parity + 1) * KB] + bias
                old = stat[n : n + 1]
                new = jnp.maximum(old, jnp.max(part, axis=0, keepdims=True))
                weights = jnp.exp(part - new)
                fade = jnp.exp(old - new)
                stat[n : n + 1] = new
                stat[4 + n : 5 + n] = stat[4 + n : 5 + n] * fade + jnp.sum(weights, axis=0, keepdims=True)
                acc[n] = acc[n] * fade + nn(turned, weights.astype(BF16))
        return carry

    lax.fori_loop(low, high, block, 0)
    lse_ref[0] = jnp.concatenate([stat[:4] + jnp.log(stat[4:]), jnp.zeros((4, 512), F32)], axis=0)
    for s in range(2):
        halves = [acc[s * 2 + n] * (1.0 / stat[4 + s * 2 + n : 5 + s * 2 + n]) for n in range(2)]
        for parity in range(2):
            for p in range(4):
                ot_ref[parity, s * 4 + p] = halves[parity][:, p * 128 : (p + 1) * 128].astype(BF16)


def smem():
    return pl.BlockSpec(memory_space=pltpu.SMEM)


def params():
    return pltpu.CompilerParams(
        vmem_limit_bytes=VMEM_LIMIT, dimension_semantics=("arbitrary",)
    )


def wide_spec():
    return pl.BlockSpec((ROWS, 1024), lambda g: (0, g))


def full_forward(lengths, ctx, query, kv):
    return pl.pallas_call(
        full_forward_kernel,
        grid=(2,),
        in_specs=[
            smem(),
            smem(),
            wide_spec(),
            pl.BlockSpec((SEQ, 128), lambda g: (0, g)),
            pl.BlockSpec((SEQ, 128), lambda g: (0, 2 + g)),
        ],
        out_specs=[
            turned_spec(),
            pl.BlockSpec((1, 8, 512), lambda g: (g, 0, 0)),
        ],
        out_shape=[
            jax.ShapeDtypeStruct((2, 16, DH, ROWS), BF16),
            jax.ShapeDtypeStruct((2, 8, 512), F32),
        ],
        scratch_shapes=[pltpu.VMEM((4, DH, 512), F32), pltpu.VMEM((8, 512), F32)],
        compiler_params=params(),
        cost_estimate=pl.CostEstimate(flops=1 << 16, bytes_accessed=1 << 16, transcendentals=0),
        name="full_forward",
    )(lengths, ctx, query, kv, kv)


def full_backward_kernel(
    len_ref, ctx_ref, q_ref, k_ref, v_ref, o_ref, g_ref, lse_ref, early_a, early_b, dq_ref, dkv_ref, acc, corr, grads
):
    first_row = ctx_ref[0, 0] * ROWS
    rows = first_row + lax.broadcasted_iota(jnp.int32, (1, ROWS), 1)
    starts = row_starts(len_ref, rows)
    low = scalar_start(len_ref, first_row) // KB
    high = (first_row + ROWS + KB - 1) // KB
    acc[...] = jnp.zeros_like(acc)
    dkv_ref[...] = jnp.zeros_like(dkv_ref)
    for s in range(2):
        for p in range(4):
            at = slice(p * 128, (p + 1) * 128)
            halves = [g_ref[parity, s * 4 + p].astype(F32) for parity in range(2)]
            grads[s, at, :] = jnp.transpose(jnp.concatenate(halves, axis=0)).astype(BF16)
            for parity in range(2):
                product = halves[parity] * o_ref[parity, s * 4 + p].astype(F32)
                n = s * 2 + parity
                corr[n : n + 1, at] = jnp.sum(product, axis=0, keepdims=True)

    def block(b, carry):
        at = pl.ds(pl.multiple_of(b * KB, KB), KB)
        bias = mask_of(starts, rows, b * KB)
        keys, values = k_ref[at, :], v_ref[at, :]
        key_terms, value_terms = [], []
        for s in range(2):
            query, grad = stacked(q_ref, s, SCALE), grads[s]
            scores = nt(both_lanes(keys, s), query)
            grad_weights = nt(both_lanes(values, s), grad)
            turned = head_transposed(keys, s)
            low_weights, grad_scores = [], []
            for parity in range(2):
                n = s * 2 + parity
                half = slice(parity * KB, (parity + 1) * KB)
                weights = jnp.exp(scores[half] + bias - lse_ref[0, n : n + 1])
                low_weights.append(weights.astype(BF16))
                term = (weights * (grad_weights[half] - corr[n : n + 1])).astype(BF16)
                grad_scores.append(term)
                acc[n] += nn(turned, term)
            key_terms.append(nn(jnp.concatenate(grad_scores, axis=0), query))
            value_terms.append(nn(jnp.concatenate(low_weights, axis=0), grad))
        dkv_ref[0, at, :128] = head_pair(*key_terms).astype(BF16)
        dkv_ref[0, at, 128:] = head_pair(*value_terms).astype(BF16)
        return carry

    lax.fori_loop(low, high, block, 0)
    for s in range(2):
        store_rows(dq_ref, jnp.concatenate([acc[s * 2], acc[s * 2 + 1]], axis=0) * SCALE, s)


def turned_spec():
    return pl.BlockSpec((2, 8, DH, ROWS), lambda g: (0, g, 0, 0))


def full_backward(lengths, ctx, query, kv, out_t, grad_t, lse, early):
    return pl.pallas_call(
        full_backward_kernel,
        grid=(2,),
        in_specs=[
            smem(),
            smem(),
            wide_spec(),
            pl.BlockSpec((SEQ, 128), lambda g: (0, g)),
            pl.BlockSpec((SEQ, 128), lambda g: (0, 2 + g)),
            turned_spec(),
            turned_spec(),
            pl.BlockSpec((1, 8, 512), lambda g: (g, 0, 0)),
            pl.BlockSpec(memory_space=pl.ANY),
            pl.BlockSpec(memory_space=pl.ANY),
        ],
        out_specs=[wide_spec(), pl.BlockSpec((1, SEQ, 256), lambda g: (g, 0, 0))],
        out_shape=[
            jax.ShapeDtypeStruct((ROWS, H * DH), BF16),
            jax.ShapeDtypeStruct((2, SEQ, 256), BF16),
        ],
        scratch_shapes=[
            pltpu.VMEM((4, DH, 512), F32),
            pltpu.VMEM((8, 512), F32),
            pltpu.VMEM((2, 512, 128), BF16),
        ],
        compiler_params=params(),
        cost_estimate=pl.CostEstimate(
            flops=1 << 16, bytes_accessed=1 << 16, transcendentals=0
        ),
        name="full_backward",
    )(lengths, ctx, query, kv, kv, out_t, grad_t, lse, *early)


def band_kernel(len_ref, ctx_ref, q_ref, k_ref, v_ref, g_ref, o_ref, dq_ref, dkv_ref):
    first_row = ctx_ref[0, 0] * ROWS
    rows = first_row + lax.broadcasted_iota(jnp.int32, (1, ROWS), 1)
    starts = jnp.maximum(row_starts(len_ref, rows), rows - (BAND - 1))
    bias = mask_of(starts, rows, first_row - BAND)
    keys, values = k_ref[...], v_ref[...]
    key_terms, value_terms = [], []
    for s in range(2):
        query, grad = stacked(q_ref, s, SCALE), stacked(g_ref, s)
        scores = nt(both_lanes(keys, s), query)
        turned = head_transposed(values, s)
        weights, low_weights, outs = [], [], []
        for parity in range(2):
            part = scores[parity * KB : (parity + 1) * KB] + bias
            grown = jnp.exp(part - jnp.max(part, axis=0, keepdims=True))
            grown = grown * (1.0 / jnp.sum(grown, axis=0, keepdims=True))
            weights.append(grown)
            low_weights.append(grown.astype(BF16))
            outs.append(nn(turned, low_weights[parity]))
        store_rows(o_ref, jnp.concatenate(outs, axis=0), s)
        corr = corrections(g_ref, o_ref, s)
        grad_weights = nt(both_lanes(values, s), grad)
        turned = head_transposed(keys, s)
        grad_scores, grad_query = [], []
        for parity in range(2):
            half = slice(parity * KB, (parity + 1) * KB)
            term = (weights[parity] * (grad_weights[half] - corr[parity])).astype(BF16)
            grad_scores.append(term)
            grad_query.append(nn(turned, term))
        store_rows(dq_ref, jnp.concatenate(grad_query, axis=0) * SCALE, s)
        key_terms.append(nn(jnp.concatenate(grad_scores, axis=0), query))
        value_terms.append(nn(jnp.concatenate(low_weights, axis=0), grad))
    dkv_ref[0, :, :128] = head_pair(*key_terms)
    dkv_ref[0, :, 128:] = head_pair(*value_terms)


def banded_layer(lengths, ctx, projected, kv_ext, grad):
    return pl.pallas_call(
        band_kernel,
        grid=(2,),
        in_specs=[
            smem(),
            smem(),
            wide_spec(),
            pl.BlockSpec((KB, 128), lambda g: (0, g)),
            pl.BlockSpec((KB, 128), lambda g: (0, 2 + g)),
            wide_spec(),
        ],
        out_specs=[wide_spec(), wide_spec(), pl.BlockSpec((1, KB, 256), lambda g: (g, 0, 0))],
        out_shape=[
            jax.ShapeDtypeStruct((ROWS, H * DH), BF16),
            jax.ShapeDtypeStruct((ROWS, H * DH), BF16),
            jax.ShapeDtypeStruct((2, KB, 256), F32),
        ],
        compiler_params=params(),
        cost_estimate=pl.CostEstimate(flops=14 * H * ROWS * KB * DH * 4, bytes_accessed=5 << 20, transcendentals=H * ROWS * KB),
        name="banded_layer",
    )(lengths, ctx, projected, kv_ext, kv_ext, grad)


def shifted(value, axis, count, step):
    return lax.ppermute(value, axis, [(i, (i + step) % count) for i in range(count)])


def swapped(value):
    return shifted(value, "c", 2, 1)


def steps_of(count):
    return sorted(range(1, count), key=lambda r: -min(r, count - r))


def sent_chunks(chunk, axis, count):
    me = lax.axis_index(axis)
    sends = [chunk(lax.rem(me + r, count)) for r in steps_of(count)]
    return sends, [shifted(send, axis, count, r) for send, r in zip(sends, steps_of(count))]


def summed(parts):
    total = parts[0].astype(F32)
    for part in parts[1:]:
        total = total + part.astype(F32)
    return total.astype(BF16)


def after(values, event):
    held, _ = lax.optimization_barrier((values, event))
    return held


def by_columns_kernel(rows_ref, early, out_ref):
    for y in range(4):
        out_ref[y] = rows_ref[:, y * 640 : (y + 1) * 640]


def by_columns(rows, early):
    return pl.pallas_call(
        by_columns_kernel,
        in_specs=[vmem(), pl.BlockSpec(memory_space=pl.ANY)],
        out_specs=vmem(),
        out_shape=jax.ShapeDtypeStruct((4, 192, 640), BF16),
        compiler_params=pltpu.CompilerParams(vmem_limit_bytes=VMEM_LIMIT),
        cost_estimate=pl.CostEstimate(flops=0, bytes_accessed=2 << 20, transcendentals=0),
        name="by_columns",
    )(rows, early)


def exchanged(value, axis, dim=0):
    return lax.all_to_all(value, axis, split_axis=dim, concat_axis=dim)


def gathered(value, axis, count):
    return exchanged(jnp.broadcast_to(value[None], (count, *value.shape)), axis)


def pick(array, index):
    return lax.dynamic_index_in_dim(array, index, 0, keepdims=False)


def nothing(values):
    first = lax.slice(values, (0,) * values.ndim, (1,) * values.ndim).reshape(())
    return jnp.minimum(jnp.abs(jnp.clip(first.astype(F32), -1.0, 1.0).astype(jnp.int32)), 0)


def gathered_round_x(piece):
    me = lax.axis_index(X)
    whole = jnp.broadcast_to(piece[:, None, None], (8, 2, 2, 8, 1536))
    for r in steps_of(4):
        source = lax.rem(me - r + 4, 4)
        part = shifted(piece, X, 4, r).reshape(8, 1, 1, 8, 1536)
        whole = lax.dynamic_update_slice(whole, part, (0, lax.rem(source, 2), lax.div(source, 2), 0, 0))
    return whole


def sent_round(value, axis, count):
    return [shifted(value, axis, count, r) for r in steps_of(count)]


def ring_sources(axis, count):
    me = lax.axis_index(axis)
    return [me] + [lax.rem(me - r + count, count) for r in steps_of(count)]


def views(refs):
    return [ref.at[i] for ref in refs for i in range(ref.shape[0])]


def weighted_kernel(count, at_ref, terms_ref, *refs):
    parts, out_ref, turned = views(refs[:count]), refs[-2], refs[-1]
    depth, width = parts[0].shape
    for i in range(8):
        mine = terms_ref[at_ref[0, i // 4], at_ref[0, 2 + i % 4]]
        turned[i, :, :depth] = jnp.transpose(mine.astype(F32)).astype(BF16)
    for tile in range(width // 256):
        at = slice(tile * 256, (tile + 1) * 256)
        total = nn(turned[0, :, :depth], parts[0][:, at])
        for i in range(1, 8):
            total = total + nn(turned[i, :, :depth], parts[i][:, at])
        out_ref[:, at] = total.astype(out_ref.dtype)


def vmem():
    return pl.BlockSpec(memory_space=pltpu.VMEM)


def weighted(at, terms, parts, dtype):
    _, depth, width = parts[0].shape
    return pl.pallas_call(
        functools.partial(weighted_kernel, len(parts)),
        in_specs=[smem()] + [vmem()] * (len(parts) + 1),
        out_specs=vmem(),
        out_shape=jax.ShapeDtypeStruct((ROWS, width), dtype),
        scratch_shapes=[pltpu.VMEM((8, ROWS, 256), BF16)],
        compiler_params=pltpu.CompilerParams(vmem_limit_bytes=VMEM_LIMIT),
        cost_estimate=pl.CostEstimate(
            flops=16 * depth * width * ROWS, bytes_accessed=16 * depth * width, transcendentals=0
        ),
        name="weighted",
    )(at, terms, *parts)


def back_through_kernel(count, at_ref, grad_ref, *refs):
    parts, out_ref = views(refs[:count]), refs[-1]
    for i in range(8):
        out_ref[at_ref[0, i // 4], at_ref[0, 2 + i % 4]] = nt(parts[i][...], grad_ref[...]).astype(out_ref.dtype)


def back_through(at, grad, parts, dtype, early):
    _, depth, width = parts[0].shape
    return pl.pallas_call(
        functools.partial(back_through_kernel, len(parts)),
        in_specs=[smem()] + [vmem()] * (len(parts) + 1) + [pl.BlockSpec(memory_space=pl.ANY)],
        out_specs=vmem(),
        out_shape=jax.ShapeDtypeStruct((2, 4, depth, ROWS), dtype),
        compiler_params=pltpu.CompilerParams(vmem_limit_bytes=VMEM_LIMIT),
        cost_estimate=pl.CostEstimate(
            flops=1 << 16, bytes_accessed=1 << 16, transcendentals=0
        ),
        name="back_through",
    )(at, grad, *parts, early)


def normalised_kernel(product_ref, resid_ref, normed_ref, rms_ref, turned_ref, scratch):
    resid = (resid_ref[...].astype(F32) + product_ref[:, :1440]).astype(BF16).astype(F32)
    rms = lax.rsqrt(jnp.sum(resid * resid, axis=1, keepdims=True) * (1.0 / 1440) + EPSILON)
    normed = resid * rms
    normed_ref[...] = normed
    rms_ref[...] = rms
    scratch[...] = jnp.transpose(jnp.concatenate([normed, jnp.zeros((ROWS, 96), F32)], axis=1))
    row = lax.broadcasted_iota(jnp.int32, (48, ROWS), 0)
    for f in range(32):
        rows = scratch[f * 45 : f * 45 + 48, :]
        turned_ref[f * 48 : (f + 1) * 48, :] = jnp.where(row < 45, rows, 0.0).astype(BF16)


def normalised(product, resid):
    return pl.pallas_call(
        normalised_kernel,
        in_specs=[vmem()] * 2,
        out_specs=[vmem()] * 3,
        out_shape=[
            jax.ShapeDtypeStruct((ROWS, 1440), F32),
            jax.ShapeDtypeStruct((ROWS, 1), F32),
            jax.ShapeDtypeStruct((1536, ROWS), BF16),
        ],
        scratch_shapes=[pltpu.VMEM((1536, ROWS), F32)],
        compiler_params=pltpu.CompilerParams(vmem_limit_bytes=VMEM_LIMIT),
        cost_estimate=pl.CostEstimate(flops=1 << 20, bytes_accessed=3 << 20, transcendentals=0),
        name="normalised",
    )(product, resid)


def through_norm_kernel(turned_ref, normed_ref, rms_ref, resid_ref, grad_ref, wide_ref, scratch):
    for f in range(32):
        scratch[f * 45 : f * 45 + 48, :] = turned_ref[f * 48 : (f + 1) * 48, :]
    scratch[1440:1536, :] = jnp.zeros((96, ROWS), F32)
    grad = jnp.transpose(scratch[...])[:, :1440]
    normed = normed_ref[...]
    middle = jnp.sum(grad * normed, axis=1, keepdims=True) * (1.0 / 1440)
    total = (resid_ref[...].astype(F32) + rms_ref[...] * (grad - normed * middle)).astype(BF16)
    grad_ref[...] = total
    wide_ref[...] = jnp.concatenate([total, jnp.zeros((ROWS, 96), BF16)], axis=1)


def through_norm(turned, normed, inverse_rms, grad_resid):
    return pl.pallas_call(
        through_norm_kernel,
        in_specs=[vmem()] * 4,
        out_specs=[vmem()] * 2,
        out_shape=[
            jax.ShapeDtypeStruct((ROWS, 1440), BF16),
            jax.ShapeDtypeStruct((ROWS, 1536), BF16),
        ],
        scratch_shapes=[pltpu.VMEM((1536, ROWS), F32)],
        compiler_params=pltpu.CompilerParams(vmem_limit_bytes=VMEM_LIMIT),
        cost_estimate=pl.CostEstimate(flops=1 << 20, bytes_accessed=3 << 20, transcendentals=0),
        name="through_norm",
    )(turned, normed, inverse_rms, grad_resid)


def column_groups(rows):
    *lead, r, width = rows.shape
    n = width // 128
    return jnp.swapaxes(rows.reshape(*lead, r, n, 128), -3, -2).reshape(*lead, n * r, 128)


def from_column_groups(groups, r):
    *lead, size, _ = groups.shape
    n = size // r
    return jnp.swapaxes(groups.reshape(*lead, n, r, 128), -3, -2).reshape(*lead, r, n * 128)


def per_device(query_a, key_a, value_a, resid_in, doc_lengths, w_out, w_qkv, grad_out, grad_resid):
    core = lax.axis_index("c")
    ctx = lax.axis_index(CTX).reshape(1, 1)
    lengths = doc_lengths
    w_b = lax.all_gather(jnp.pad(w_qkv, ((0, 3), (0, 0))), FSDP, axis=0, tiled=True)
    eighth = jnp.pad(pick(w_out.reshape(8, 8, 1440), lax.axis_index(CTX)), ((0, 0), (0, 96)))
    out_piece = gathered_round_x(gathered(eighth, "z", 8))
    out_parts = sent_round(out_piece, "y", 4)
    own_kv = jnp.concatenate([key_a[0], value_a[0]], axis=1)
    own_kv = jnp.where(nothing(out_piece) == 0, own_kv, jnp.zeros_like(own_kv))
    kv = gathered(own_kv, CTX, 8).reshape(SEQ, 512)
    query = query_a[0]
    attended_t, lse = full_forward(lengths, ctx, query, kv)
    own_o = [part.reshape(1, 256, 1536) for part in [out_piece, *out_parts]]
    other_o = [swapped(part) for part in own_o]
    both_o = own_o + other_o
    at_y = jnp.stack([core, 1 - core, *ring_sources("y", 4)]).astype(jnp.int32).reshape(1, 6)
    attended_t = attended_t.reshape(2, 1024, ROWS)
    own_t, other_t = pick(attended_t, core), pick(attended_t, 1 - core)
    pair_attended = jnp.concatenate([own_t, swapped(other_t)], axis=1)
    by_y = attended_t.reshape(2, 8, 2, 2, 4, 8, ROWS).transpose(0, 4, 1, 2, 3, 5, 6).reshape(2, 4, 256, ROWS)
    product = weighted(at_y, by_y, both_o, F32)
    normed, inverse_rms, padded = normalised(product, resid_in[0])
    turned = padded
    turned = turned.reshape(8, 2, 2, 2, 24, ROWS).transpose(2, 3, 1, 0, 4, 5).reshape(2, 768, ROWS)
    own_n = pick(turned, core)
    sent_normed = pick(turned, 1 - core)
    pair_normed = jnp.concatenate([own_n, swapped(sent_normed)], axis=1)
    projected = tn(padded, w_b).astype(BF16)
    own_b = projected[:, H * DH :]
    tail = shifted(own_b, CTX, 8, 1)
    kv_ext = jnp.concatenate([tail, own_b], axis=0)
    banded, grad_qb, kv_grad = banded_layer(lengths, ctx, projected, kv_ext, grad_out[0])
    head = shifted(kv_grad[:, :BAND].astype(BF16), CTX, 8, -1).astype(F32)
    swapped_qb = swapped(grad_qb)
    grad_turned = nt(w_b[:, : H * DH], grad_qb)
    last = lax.axis_index(CTX) + nothing(grad_turned) == 7
    own_grad = (kv_grad[:, BAND:] + jnp.where(last, 0.0, head)).astype(BF16)
    grad_kvb = jnp.concatenate(
        [own_grad[0, :, :128], own_grad[1, :, :128], own_grad[0, :, 128:], own_grad[1, :, 128:]], axis=1
    )
    pair_kvb = jnp.concatenate([grad_kvb, swapped(grad_kvb)], axis=0)
    grad_turned = grad_turned + nt(w_b[:, H * DH :], grad_kvb)
    grad_mid, wide_mid = through_norm(grad_turned, normed, inverse_rms, grad_resid[0])
    pair_mid = jnp.concatenate([wide_mid, swapped(wide_mid)], axis=0)
    sent_out = jnp.stack([nn(pair_attended, pair_mid[:, y * 384 : (y + 1) * 384]).astype(BF16) for y in range(4)])
    me_y = lax.axis_index("y")
    out_sends = [pick(sent_out, lax.rem(me_y + r, 4)) for r in steps_of(4)]
    out_first = [shifted(send, "y", 4, r) for send, r in zip(out_sends, steps_of(4))]
    out_first.append(pick(sent_out, me_y))
    pair_proj = jnp.concatenate([jnp.concatenate([grad_qb, swapped_qb], axis=0), pair_kvb], axis=1)
    pair_proj = jnp.where(nothing(sent_out) == 0, pair_proj, jnp.zeros_like(pair_proj))
    first = nn(pair_normed, pair_proj).astype(BF16).reshape(4, 192, 2560)
    first_sent = first
    first = lax.psum_scatter(first, X, scatter_dimension=0, tiled=False)
    grad_t = back_through(at_y, wide_mid, both_o, BF16, out_sends[-1])
    grad_t = grad_t.reshape(2, 4, 8, 2, 2, 8, ROWS).transpose(0, 2, 3, 4, 1, 5, 6)
    grad_query, kv_terms = full_backward(
        lengths, ctx, query, kv, attended_t.reshape(2, 16, DH, ROWS), grad_t.reshape(2, 16, DH, ROWS), lse, [first_sent, out_sends[-1]]
    )
    kv_terms = exchanged(kv_terms.reshape(2, 8, ROWS, 256), CTX, 1)
    out_first = summed(out_first).reshape(8, 2, 2, 32, 384).transpose(2, 1, 0, 3, 4).reshape(4, 256, 384)
    first = by_columns(first.reshape(192, 2560), out_first)
    _, second = sent_chunks(lambda i: pick(first, i), "y", 4)
    second.append(pick(first, lax.axis_index("y")))
    _, out_second = sent_chunks(lambda i: pick(out_first, i), X, 4)
    out_second.append(pick(out_first, lax.axis_index(X) + nothing(kv_terms)))
    own_terms = jnp.sum(kv_terms.astype(F32), axis=1).astype(BF16)
    grad_key = jnp.concatenate([own_terms[0, :, :128], own_terms[1, :, :128]], axis=1)
    grad_value = jnp.concatenate([own_terms[0, :, 128:], own_terms[1, :, 128:]], axis=1)
    both = jnp.concatenate(
        [
            column_groups(summed(second).reshape(8, 24, 640)),
            column_groups(summed(out_second).reshape(8, 32, 384)),
        ],
        axis=1,
    )
    both = exchanged(both, "z")
    both = jnp.sum(both.astype(F32), axis=0).astype(BF16)
    both = gathered(both, CTX, 8)
    qkv_rows = from_column_groups(both[:, :120], 24).reshape(2, 4, 24, 640)
    grad_w_qkv = qkv_rows.transpose(0, 2, 1, 3).reshape(48, 2560)[:45].astype(F32)
    out_rows = from_column_groups(both[:, 120:], 32).reshape(2, 4, 32, 384)
    grad_w_out = out_rows.transpose(0, 2, 1, 3).reshape(64, 1536)[:, :1440].astype(F32)
    return (
        banded[None],
        grad_mid[None],
        grad_query[None],
        grad_key[None],
        grad_value[None],
        grad_w_out,
        grad_w_qkv,
    )


def solution(mesh):
    torus = jax.sharding.Mesh(mesh.devices.reshape(2, 4, 8, 2, 2), ("xh", "y", "z", "xl", "c"))
    rows = P(FSDP, CTX, None)
    weight = P(FSDP, None)
    return jax.shard_map(
        per_device,
        mesh=torus,
        in_specs=(rows, rows, rows, rows, weight, weight, weight, rows, rows),
        out_specs=(rows, rows, rows, rows, rows, weight, weight),
        check_vma=False,
    )
```
